128 devices in a mesh: comp: 2 (over core), dom: 64 (over y, x, z).
Axes of the slice: x: 4, y: 4, z: 4, core: 2. Of those that a mesh axis runs over, the one named last changes fastest.
Arguments:
- model_state: float32 [2, 4, 16, 262144], P('comp', None, None, 'dom'), may hold values from -6 to 6
- neighbours: int32 [2, 8, 262144], P('comp', None, 'dom'), may hold values from 0 to 512, as said below
- stencil_coef: float32 [2, 8, 262144], P('comp', None, 'dom'), may hold values from 0.02 to 0.12
- column_mixing_operator: float32 [2, 16, 16], P('comp'), may hold values from -1.5 to 1.5
- remap_count: int32 [2, 64, 64], P('comp', 'dom'), may hold values from 256 to 1024, as said below
- remap_source: int32 [2, 64, 64, 1024], P('comp', 'dom'), may hold values from 0 to 4095
- remap_weight: float32 [2, 64, 64, 1024], P('comp', 'dom'), may hold values from 0.1 to 1
- remap_target: int32 [2, 64, 64, 1024], P('comp', 'dom'), may hold values from 0 to 4095
Outputs:
- updated_state: float32 [2, 4, 16, 262144], P('comp', None, None, 'dom')
- interface_flux_fields: float32 [2, 4, 262144], P('comp', None, 'dom')
The draws below stay inside these ranges and needn't reach their ends.
Inputs may be any that keep to these rules, and one draw needn't show every extreme that they name: `neighbours`: in every partition's block some cell has an entry 0 and some an entry 512. remap_count[s, p, q] slots of partition p of section s go to partition q of the other section; every sender and every receiver has at least one pair with 1024 used slots.
All inputs are finite; a program needn't handle non-finite values.
Results may differ from the reference program's by a relative error of at most 0.0001.
Values sent between devices are 32-bit elements; how exact they have to be, the bound alone decides.
A program may use at most 256 MiB of HBM per device.

```python
import jax
import jax.numpy as jnp
from jax import lax

VARS = 4
LEV = 16
NBR = 8
CELLS_DEV = 4096
CAP = 1024
HALO = 256
PEERS = 64
CELLS = 262144


def draw_neighbours(key, part):
    entries = jax.random.randint(key, (2, NBR, CELLS), 0, 2 * HALO + 1)
    cell_index = jnp.arange(CELLS, dtype=jnp.int32)
    local_index = cell_index % CELLS_DEV
    first_row = (jnp.arange(NBR) == 0)[None, :, None]
    entries = jnp.where(first_row & (local_index == 0)[None, None, :], 0, entries)
    entries = jnp.where(first_row & (local_index == CELLS_DEV - 1)[None, None, :], 2 * HALO, entries)
    return entries.astype(jnp.int32)


def draw_remap_count(key, part):
    counts_drawn = jax.random.randint(key, (2, PEERS, PEERS), CAP // 4, CAP + 1)
    rotation = jax.random.randint(jax.random.fold_in(key, 1), (2,), 0, PEERS)
    senders = jnp.arange(PEERS, dtype=jnp.int32)
    clipped_state = (senders[None, :, None] + rotation[:, None, None]) % PEERS == senders[None, None, :]
    return jnp.where(clipped_state, CAP, counts_drawn).astype(jnp.int32)


def plant(drawn, own_key, least, high):
    index_at = [jax.random.randint(jax.random.fold_in(own_key, axis), (), 0, length) for axis, length in enumerate(drawn.shape)]
    widest = drawn.shape.index(max(drawn.shape))
    beside = index_at[:widest] + [(index_at[widest] + 1) % drawn.shape[widest]] + index_at[widest + 1:]
    return drawn.at[tuple(index_at)].set(least).at[tuple(beside)].set(high)


def steps_of(rng, shape, split, low, high):
    def one(position, shards_of):
        steps = jax.random.uniform(jax.random.fold_in(jax.random.fold_in(rng, 6), position), (shards_of,), jnp.float32, low / len(split), high / len(split))
        return jnp.repeat(jnp.exp(steps), shape[position] // shards_of).reshape((-1,) + (1,) * (len(shape) - position - 1))

    level = one(*split[0])
    for cut in split[1:]:
        level = level * one(*cut)
    return level


def gaussian(key, dims, deviation, most, shards=(), kind=jnp.bfloat16):
    values = jax.random.normal(key, dims, jnp.float32) * deviation
    if len(shards) > 0:
        values = steps_of(key, dims, shards, -0.22, 0.18) * values
    return jnp.clip(values, min=-most, max=most).astype(kind)


def setup_inputs(seed: int = 0) -> dict:
    seeds = jax.random.split(jax.random.key(seed), 9)
    return {
        "model_state": gaussian(seeds[0], (2, VARS, LEV, CELLS), 1.0, 6.0, ((0, 2), (3, 64)), jnp.float32),
        "neighbours": draw_neighbours(jax.random.fold_in(seeds[8], 71), 0),
        "stencil_coef": jnp.clip(0.02 + 0.09999999776482582 * jax.random.uniform(seeds[2], (2, NBR, CELLS), jnp.float32) ** steps_of(seeds[2], (2, NBR, CELLS), ((0, 2), (2, 64)), -0.2, 0.2), 0.02, 0.12),
        "column_mixing_operator": gaussian(seeds[3], (2, LEV, LEV), LEV ** -0.5, 1.5, ((0, 2),), jnp.float32),
        "remap_count": draw_remap_count(jax.random.fold_in(seeds[8], 71), 0),
        "remap_source": plant(jax.random.randint(seeds[5], (2, PEERS, PEERS, CAP), 0, CELLS_DEV), jax.random.fold_in(seeds[5], 1), 0, CELLS_DEV - 1).astype(jnp.int32),
        "remap_weight": jnp.clip(0.1 + 0.9 * jax.random.uniform(seeds[6], (2, PEERS, PEERS, CAP), jnp.float32) ** steps_of(seeds[6], (2, PEERS, PEERS, CAP), ((0, 2), (1, 64)), -0.2, 0.2), 0.1, 1.0),
        "remap_target": plant(jax.random.randint(seeds[7], (2, PEERS, PEERS, CAP), 0, CELLS_DEV), jax.random.fold_in(seeds[7], 1), 0, CELLS_DEV - 1).astype(jnp.int32),
    }


def reference(model_state, neighbours, stencil_coef, column_mixing_operator, remap_count, remap_source, remap_weight, remap_target):
    export = model_state[:, :, 0, :]
    slot_index = jnp.arange(CAP, dtype=jnp.int32)
    offsets_peer = (jnp.arange(PEERS, dtype=jnp.int32) * CELLS_DEV)[:, None, None]
    imports = []
    for receiver in range(2):
        sender = 1 - receiver
        source_cells = (remap_source[sender] + offsets_peer).astype(jnp.int32)
        values = jnp.take(export[sender], source_cells.reshape(-1), axis=1).reshape(VARS, PEERS, PEERS, CAP)
        occupied = slot_index[None, None, :] < remap_count[sender][:, :, None]
        weighted = jnp.where(occupied[None], remap_weight[sender][None] * values, jnp.zeros((), jnp.float32))
        target_cells = (remap_target[receiver] + offsets_peer).astype(jnp.int32)
        target_cells = jnp.transpose(target_cells, (1, 0, 2))
        imported = jnp.zeros((VARS, CELLS), jnp.float32).at[:, target_cells.reshape(-1)].add(weighted.reshape(VARS, -1))
        imports.append(imported)
    coupled = jnp.stack(imports)
    cell_index = jnp.arange(CELLS, dtype=jnp.int32)
    results = []
    for domain_section in range(2):
        current = model_state[domain_section]
        lateral = jnp.zeros_like(current)
        for neighbour in range(NBR):
            target = ((cell_index + neighbours[domain_section, neighbour] - HALO) % CELLS).astype(jnp.int32)
            adjacent_section = jnp.take(current, target, axis=2)
            lateral = lateral + stencil_coef[domain_section, neighbour][None, None, :] * (adjacent_section - current)
        forcing_applied = current + lateral
        forcing_applied = forcing_applied.at[:, 0, :].add(coupled[domain_section])
        advanced_state = jnp.einsum("bx,exz->ebz", column_mixing_operator[domain_section], forcing_applied, precision=lax.Precision.HIGHEST)
        results.append(advanced_state)
    return jnp.stack(results), coupled
```

```python
import functools

import jax
import jax.numpy as jnp
from jax import lax
from jax.experimental import pallas as pl
from jax.experimental.pallas import tpu as pltpu
from jax.sharding import PartitionSpec as P

MESH = pl.DeviceIdType.MESH
F32, BF16, I32, I16 = jnp.float32, jnp.bfloat16, jnp.int32, jnp.int16
LANES = 128
SIDE = 4
PEERS = SIDE**3
VARS, LEV, NBR = 4, 16, 8
CELLS = 4096
CAP = 1024
HALO = 256
BLOCKS = CELLS // LANES
CHUNKS = CAP // LANES
ROWS = VARS * LEV
FROM_LEFT, FROM_RIGHT = 0, HALO + CELLS


def halves(x):
    high = x.astype(BF16)
    return high, (x - high.astype(F32)).astype(BF16)


def lane_pick(table, index):
    return jnp.take_along_axis(table, index, axis=1, mode="promise_in_bounds")


def sublane_pick(table, index):
    return jnp.take_along_axis(table, index, axis=0, mode="promise_in_bounds")


def peer_at(me, step, sign):
    place = 0
    for unit in (16, 4, 1):
        at = lax.rem(lax.div(me, unit), SIDE)
        move = lax.rem(lax.div(step, unit), SIDE)
        place = place + unit * lax.rem(at + sign * move + SIDE, SIDE)
    return place


def kernel(
    state_hbm,
    neighbours_hbm,
    coef_hbm,
    mixing_ref,
    count_ref,
    source_hbm,
    weight_hbm,
    target_hbm,
    mixed_hbm,
    flux_ref,
    ext,
    nbr,
    coef,
    raw_source,
    raw_weight,
    raw_target,
    source,
    weight,
    target,
    table,
    sendbuf,
    recvbuf,
    mixed,
    total,
    in_sems,
    halo_send_sems,
    halo_recv_sems,
    send_sems,
    recv_sems,
    out_sem,
):
    comp, me = lax.axis_index("comp"), lax.axis_index("dom")
    other = 1 - comp
    right, left = lax.rem(me + 1, PEERS), lax.rem(me + PEERS - 1, PEERS)

    loads = [
        pltpu.make_async_copy(src, dst, in_sems.at[i])
        for i, (src, dst) in enumerate(
            (
                (state_hbm.at[0], ext.at[:, :, pl.ds(HALO, CELLS)]),
                (source_hbm.at[0, 0], raw_source),
                (weight_hbm.at[0, 0], raw_weight),
                (neighbours_hbm.at[0], nbr),
                (coef_hbm.at[0], coef),
                (target_hbm.at[0, 0], raw_target),
            )
        )
    ]
    for load in loads:
        load.start()

    barrier = pltpu.get_barrier_semaphore()

    def greet(step, c):
        pl.semaphore_signal(barrier, inc=1, device_id=(other, step), device_id_type=MESH)
        return c

    lax.fori_loop(0, PEERS, greet, 0)
    for side in (left, right):
        pl.semaphore_signal(barrier, inc=1, device_id=(comp, side), device_id_type=MESH)

    loads[0].wait()
    for v in range(VARS):
        for b in range(BLOCKS):
            table[v * BLOCKS + b : v * BLOCKS + b + 1, :] = ext[
                v, 0:1, HALO + b * LANES : HALO + (b + 1) * LANES
            ]
    table_halves = jnp.concatenate(halves(table[...]), axis=1)

    loads[1].wait()
    loads[2].wait()

    def by_peer(raw, tidy):
        for g in range(PEERS // 8):
            for c in range(CHUNKS):
                tidy[pl.ds(g * 8 * CHUNKS + c, 8, stride=CHUNKS), :] = raw[
                    g * 8 : g * 8 + 8, c * LANES : (c + 1) * LANES
                ]

    by_peer(raw_source, source)
    by_peer(raw_weight, weight)

    pl.semaphore_wait(barrier, PEERS + 2)

    halos = [
        pltpu.make_async_remote_copy(
            src_ref=state_hbm.at[0, :, :, pl.ds(start, HALO)],
            dst_ref=ext.at[:, :, pl.ds(place, HALO)],
            send_sem=halo_send_sems.at[i],
            recv_sem=halo_recv_sems.at[i],
            device_id=(comp, side),
            device_id_type=MESH,
        )
        for i, (start, place, side) in enumerate(
            ((CELLS - HALO, FROM_LEFT, right), (0, FROM_RIGHT, left))
        )
    ]
    for halo in halos:
        halo.start()

    sublane = lax.broadcasted_iota(I32, (8, LANES), 0)
    lane = lax.broadcasted_iota(I32, (8, LANES), 1)
    slot = sublane * LANES + lane
    lane_rows = lax.broadcasted_iota(I32, (LANES, 1), 0).astype(I16)
    block_rows = lax.broadcasted_iota(I32, (BLOCKS, 1), 0).astype(I16)
    one, nought = BF16(1), BF16(0)

    def to_peer(q):
        return pltpu.make_async_remote_copy(
            src_ref=sendbuf.at[q],
            dst_ref=recvbuf.at[me],
            send_sem=send_sems.at[q],
            recv_sem=recv_sems.at[me],
            device_id=(other, q),
            device_id_type=MESH,
        )

    def from_peer(p):
        return pltpu.make_async_remote_copy(
            src_ref=sendbuf.at[p],
            dst_ref=recvbuf.at[p],
            send_sem=send_sems.at[p],
            recv_sem=recv_sems.at[p],
            device_id=(other, p),
            device_id_type=MESH,
        )

    def gather(step, c_):
        q = peer_at(me, step, 1)
        cells = source[pl.ds(pl.multiple_of(q * CHUNKS, CHUNKS), CHUNKS), :]
        low, high = cells & (LANES - 1), cells >> 7
        used = jnp.where(
            slot < count_ref[0, 0, q],
            weight[pl.ds(pl.multiple_of(q * CHUNKS, CHUNKS), CHUNKS), :],
            0.0,
        )
        out = [jnp.zeros((8, LANES), F32) for _ in range(VARS)]
        for n in range(CHUNKS // 2):
            lows = jnp.concatenate([low[2 * n : 2 * n + 1], low[2 * n + 1 : 2 * n + 2]], axis=1)
            hot = jnp.where(lane_rows == lows.astype(I16), one, nought)
            rows = jnp.dot(
                table_halves,
                jnp.concatenate([hot, hot], axis=0),
                preferred_element_type=F32,
            )
            for half in range(2):
                c = 2 * n + half
                row = jnp.broadcast_to(high[c : c + 1], (8, LANES))
                within, group = row & 7, row >> 3
                for v in range(VARS):
                    picks = [
                        sublane_pick(
                            rows[
                                v * BLOCKS + t * 8 : v * BLOCKS + t * 8 + 8,
                                half * LANES : (half + 1) * LANES,
                            ],
                            within,
                        )
                        for t in range(BLOCKS // 8)
                    ]
                    pick = jnp.where(
                        group < 2,
                        jnp.where(group == 0, picks[0], picks[1]),
                        jnp.where(group == 2, picks[2], picks[3]),
                    )
                    out[v] = jnp.where(sublane == c, pick, out[v])
        for v in range(VARS):
            sendbuf[q, v * 8 : v * 8 + 8, :] = out[v] * used
        to_peer(q).start()
        return c_

    lax.fori_loop(0, PEERS, gather, 0)

    spread = (
        lax.rem(lax.broadcasted_iota(I32, (ROWS, LEV), 0), LEV)
        == lax.broadcasted_iota(I32, (ROWS, LEV), 1)
    ).astype(F32)
    tiled = lax.dot_general(
        jnp.dot(spread, mixing_ref[0], precision=lax.Precision.HIGHEST, preferred_element_type=F32),
        spread,
        (((1,), (1,)), ((), ())),
        precision=lax.Precision.HIGHEST,
        preferred_element_type=F32,
    )
    same = lax.div(lax.broadcasted_iota(I32, (ROWS, ROWS), 0), LEV) == lax.div(
        lax.broadcasted_iota(I32, (ROWS, ROWS), 1), LEV
    )
    mix_high, mix_low = halves(jnp.where(same, tiled, 0.0))
    mix_high = jnp.concatenate([mix_high, mix_high], axis=1)
    mix_low = jnp.concatenate([mix_low, mix_low], axis=1)

    loads[3].wait()
    loads[4].wait()
    for halo in halos:
        halo.wait_recv()

    def stencil(b, c_):
        base = pl.multiple_of(b * LANES, LANES)
        near = nbr[:, pl.ds(base, LANES)]
        coefs = coef[:, pl.ds(base, LANES)]

        def rows(r, s):
            return ext[r // 2, (r % 2) * 8 : (r % 2) * 8 + 8, pl.ds(base + s * LANES, LANES)]

        now = [rows(r, 2) for r in range(ROWS // 8)]
        acc = list(now)
        for j in range(NBR):
            place = lane + near[j : j + 1]
            at, block = place & (LANES - 1), place >> 7
            factor = jnp.broadcast_to(coefs[j : j + 1], (8, LANES))
            for r in range(ROWS // 8):
                pick = lane_pick(rows(r, 0), at)
                for s in range(1, 5):
                    pick = jnp.where(block == s, lane_pick(rows(r, s), at), pick)
                acc[r] = acc[r] + factor * (pick - now[r])
        high, low = halves(jnp.concatenate(acc, axis=0))
        both = jnp.concatenate([high, low], axis=0)
        result = jnp.dot(mix_high, both, preferred_element_type=F32) + jnp.dot(
            mix_low, both, preferred_element_type=F32
        )
        for v in range(VARS):
            mixed[v, :, pl.ds(base, LANES)] = result[v * LEV : (v + 1) * LEV]
        return c_

    lax.fori_loop(0, BLOCKS, stencil, 0)
    store = pltpu.make_async_copy(mixed, mixed_hbm, out_sem)
    store.start()

    loads[5].wait()
    by_peer(raw_target, target)
    total[...] = jnp.zeros_like(total)

    def scatter(step, c_):
        p = peer_at(me, step, -1)
        from_peer(p).wait_recv()
        cells = target[pl.ds(pl.multiple_of(p * CHUNKS, CHUNKS), CHUNKS), :]
        low, high = (cells & (LANES - 1)), (cells >> 7)
        values, hots = [], []
        for c in range(CHUNKS):
            here = block_rows == high[c : c + 1].astype(I16)
            hots.append(jnp.where(lane_rows == low[c : c + 1].astype(I16), one, nought))
            parts = [halves(recvbuf[p, v * 8 + c : v * 8 + c + 1, :]) for v in range(VARS)]
            values.append(
                jnp.concatenate(
                    [jnp.where(here, parts[v][i], nought) for i in range(2) for v in range(VARS)],
                    axis=0,
                )
            )
        total[...] += lax.dot_general(
            jnp.concatenate(values, axis=1),
            jnp.concatenate(hots, axis=1),
            (((1,), (1,)), ((), ())),
            preferred_element_type=F32,
        )
        return c_

    lax.fori_loop(0, PEERS, scatter, 0)

    for v in range(VARS):
        for b in range(BLOCKS):
            r = v * BLOCKS + b
            flux_ref[v : v + 1, b * LANES : (b + 1) * LANES] = (
                total[r : r + 1, :] + total[r + VARS * BLOCKS : r + VARS * BLOCKS + 1, :]
            )

    def sent(step, c_):
        to_peer(step).wait_send()
        return c_

    lax.fori_loop(0, PEERS, sent, 0)
    for halo in halos:
        halo.wait_send()
    store.wait()


def local(
    model_state,
    neighbours,
    stencil_coef,
    column_mixing_operator,
    remap_count,
    remap_source,
    remap_weight,
    remap_target,
):
    hbm = pl.BlockSpec(memory_space=pltpu.HBM)
    vmem = pl.BlockSpec(memory_space=pltpu.VMEM)
    smem = pl.BlockSpec(memory_space=pltpu.SMEM)
    mixed, flux = pl.pallas_call(
        kernel,
        out_shape=(
            jax.ShapeDtypeStruct((VARS, LEV, CELLS), F32),
            jax.ShapeDtypeStruct((VARS, CELLS), F32),
        ),
        in_specs=[hbm, hbm, hbm, vmem, smem, hbm, hbm, hbm],
        out_specs=(hbm, vmem),
        scratch_shapes=[
            pltpu.VMEM((VARS, LEV, CELLS + 2 * HALO), F32),
            pltpu.VMEM((NBR, CELLS), I32),
            pltpu.VMEM((NBR, CELLS), F32),
            pltpu.VMEM((PEERS, CAP), I32),
            pltpu.VMEM((PEERS, CAP), F32),
            pltpu.VMEM((PEERS, CAP), I32),
            pltpu.VMEM((PEERS * CHUNKS, LANES), I32),
            pltpu.VMEM((PEERS * CHUNKS, LANES), F32),
            pltpu.VMEM((PEERS * CHUNKS, LANES), I32),
            pltpu.VMEM((VARS * BLOCKS, LANES), F32),
            pltpu.VMEM((PEERS, VARS * CHUNKS, LANES), F32),
            pltpu.VMEM((PEERS, VARS * CHUNKS, LANES), F32),
            pltpu.VMEM((VARS, LEV, CELLS), F32),
            pltpu.VMEM((2 * VARS * BLOCKS, LANES), F32),
            pltpu.SemaphoreType.DMA((6,)),
            pltpu.SemaphoreType.DMA((2,)),
            pltpu.SemaphoreType.DMA((2,)),
            pltpu.SemaphoreType.DMA((PEERS,)),
            pltpu.SemaphoreType.DMA((PEERS,)),
            pltpu.SemaphoreType.DMA,
        ],
        compiler_params=pltpu.CompilerParams(
            collective_id=0, has_side_effects=True, vmem_limit_bytes=32 << 20
        ),
        name="step",
    )(
        model_state,
        neighbours,
        stencil_coef,
        column_mixing_operator,
        remap_count,
        remap_source,
        remap_weight,
        remap_target,
    )
    updated = mixed + column_mixing_operator[0, :, 0][None, :, None] * flux[:, None, :]
    return updated[None], flux[None]


def solution(mesh):
    in_specs = (
        P("comp", None, None, "dom"),
        P("comp", None, "dom"),
        P("comp", None, "dom"),
        P("comp", None, None),
        P("comp", "dom", None),
        P("comp", "dom", None, None),
        P("comp", "dom", None, None),
        P("comp", "dom", None, None),
    )
    out_specs = (P("comp", None, None, "dom"), P("comp", None, "dom"))
    return jax.shard_map(local, mesh=mesh, in_specs=in_specs, out_specs=out_specs, check_vma=False)
```

```python
import functools

import jax
import jax.numpy as jnp
from jax import lax
from jax.experimental import pallas as pl
from jax.experimental.pallas import tpu as pltpu
from jax.sharding import PartitionSpec as P

MESH = pl.DeviceIdType.MESH
F32, BF16, I32, I16 = jnp.float32, jnp.bfloat16, jnp.int32, jnp.int16
LANES = 128
SIDE = 4
PEERS = SIDE**3
VARS, LEV, NBR = 4, 16, 8
CELLS = 4096
CAP = 1024
HALO = 256
BLOCKS = CELLS // LANES
CHUNKS = CAP // LANES
ROWS = VARS * LEV
SPAN = 2 * HALO // LANES + 1
GU, SU, STU = 8, 8, 4
FROM_LEFT, FROM_RIGHT = 0, HALO + CELLS


def halves(x):
    high = x.astype(BF16)
    return high, (x - high.astype(F32)).astype(BF16)


def lane_pick(table, index):
    return jnp.take_along_axis(table, index, axis=1, mode="promise_in_bounds")


def sublane_pick(table, index):
    return jnp.take_along_axis(table, index, axis=0, mode="promise_in_bounds")


def peer_at(me, step, sign):
    place = 0
    for unit in (16, 4, 1):
        at = lax.rem(lax.div(me, unit), SIDE)
        move = lax.rem(lax.div(step, unit), SIDE)
        place = place + unit * lax.rem(at + sign * move + SIDE, SIDE)
    return place


def kernel(
    state_hbm,
    neighbours_hbm,
    coef_hbm,
    mixing_ref,
    count_ref,
    source_hbm,
    weight_hbm,
    target_hbm,
    mixed_hbm,
    flux_ref,
    ext,
    nbr,
    coef,
    raw_source,
    raw_weight,
    raw_target,
    source,
    weight,
    target,
    table,
    sendbuf,
    recvbuf,
    split,
    forced,
    mixed,
    total,
    in_sems,
    halo_send_sems,
    halo_recv_sems,
    send_sems,
    recv_sems,
    out_sem,
):
    comp, me = lax.axis_index("comp"), lax.axis_index("dom")
    other = 1 - comp
    right, left = lax.rem(me + 1, PEERS), lax.rem(me + PEERS - 1, PEERS)

    loads = [
        pltpu.make_async_copy(src, dst, in_sems.at[i])
        for i, (src, dst) in enumerate(
            (
                (state_hbm.at[0], ext.at[:, :, pl.ds(HALO, CELLS)]),
                (source_hbm.at[0, 0], raw_source),
                (weight_hbm.at[0, 0], raw_weight),
                (neighbours_hbm.at[0], nbr),
                (coef_hbm.at[0], coef),
                (target_hbm.at[0, 0], raw_target),
            )
        )
    ]
    for load in loads:
        load.start()

    barrier = pltpu.get_barrier_semaphore()

    def greet(step, c):
        pl.semaphore_signal(barrier, inc=1, device_id=(other, step), device_id_type=MESH)
        return c

    lax.fori_loop(0, PEERS, greet, 0)
    for side in (left, right):
        pl.semaphore_signal(barrier, inc=1, device_id=(comp, side), device_id_type=MESH)

    loads[0].wait()
    for v in range(VARS):
        for b in range(BLOCKS):
            table[v * BLOCKS + b : v * BLOCKS + b + 1, :] = ext[
                v, 0:1, HALO + b * LANES : HALO + (b + 1) * LANES
            ]
    table_halves = jnp.concatenate(halves(table[...]), axis=1)

    loads[1].wait()
    loads[2].wait()

    def by_peer(raw, tidy):
        for g in range(PEERS // 8):
            for c in range(CHUNKS):
                tidy[pl.ds(g * 8 * CHUNKS + c, 8, stride=CHUNKS), :] = raw[
                    g * 8 : g * 8 + 8, c * LANES : (c + 1) * LANES
                ]

    by_peer(raw_source, source)
    by_peer(raw_weight, weight)

    pl.semaphore_wait(barrier, PEERS + 2)

    halos = [
        pltpu.make_async_remote_copy(
            src_ref=state_hbm.at[0, :, :, pl.ds(start, HALO)],
            dst_ref=ext.at[:, :, pl.ds(place, HALO)],
            send_sem=halo_send_sems.at[i],
            recv_sem=halo_recv_sems.at[i],
            device_id=(comp, side),
            device_id_type=MESH,
        )
        for i, (start, place, side) in enumerate(
            ((CELLS - HALO, FROM_LEFT, right), (0, FROM_RIGHT, left))
        )
    ]
    for halo in halos:
        halo.start()

    sublane = lax.broadcasted_iota(I32, (8, LANES), 0)
    lane = lax.broadcasted_iota(I32, (8, LANES), 1)
    slot = sublane * LANES + lane
    lane_rows = lax.broadcasted_iota(I32, (LANES, 1), 0).astype(I16)
    block_rows = lax.broadcasted_iota(I32, (BLOCKS, 1), 0).astype(I16)
    one, nought = BF16(1), BF16(0)

    def to_peer(q):
        return pltpu.make_async_remote_copy(
            src_ref=sendbuf.at[q],
            dst_ref=recvbuf.at[me],
            send_sem=send_sems.at[q],
            recv_sem=recv_sems.at[me],
            device_id=(other, q),
            device_id_type=MESH,
        )

    def from_peer(p):
        return pltpu.make_async_remote_copy(
            src_ref=sendbuf.at[p],
            dst_ref=recvbuf.at[p],
            send_sem=send_sems.at[p],
            recv_sem=recv_sems.at[p],
            device_id=(other, p),
            device_id_type=MESH,
        )

    def gather(step, c_):
        q = peer_at(me, step, 1)
        cells = source[pl.ds(pl.multiple_of(q * CHUNKS, CHUNKS), CHUNKS), :]
        low, high = cells & (LANES - 1), cells >> 7
        used = jnp.where(
            slot < count_ref[0, 0, q],
            weight[pl.ds(pl.multiple_of(q * CHUNKS, CHUNKS), CHUNKS), :],
            0.0,
        )
        out = [jnp.zeros((8, LANES), F32) for _ in range(VARS)]
        for n in range(CHUNKS // 2):
            lows = jnp.concatenate([low[2 * n : 2 * n + 1], low[2 * n + 1 : 2 * n + 2]], axis=1)
            hot = jnp.where(lane_rows == lows.astype(I16), one, nought)
            rows = jnp.dot(
                table_halves,
                jnp.concatenate([hot, hot], axis=0),
                preferred_element_type=F32,
            )
            for half in range(2):
                c = 2 * n + half
                row = jnp.broadcast_to(high[c : c + 1], (8, LANES))
                within, group = row & 7, row >> 3
                for v in range(VARS):
                    picks = [
                        sublane_pick(
                            rows[
                                v * BLOCKS + t * 8 : v * BLOCKS + t * 8 + 8,
                                half * LANES : (half + 1) * LANES,
                            ],
                            within,
                        )
                        for t in range(BLOCKS // 8)
                    ]
                    pick = jnp.where(
                        group < 2,
                        jnp.where(group == 0, picks[0], picks[1]),
                        jnp.where(group == 2, picks[2], picks[3]),
                    )
                    out[v] = jnp.where(sublane == c, pick, out[v])
        for v in range(VARS):
            sendbuf[q, v * 8 : v * 8 + 8, :] = out[v] * used
        to_peer(q).start()
        return c_

    lax.fori_loop(0, PEERS, gather, 0, unroll=GU)

    spread = (
        lax.rem(lax.broadcasted_iota(I32, (ROWS, LEV), 0), LEV)
        == lax.broadcasted_iota(I32, (ROWS, LEV), 1)
    ).astype(F32)
    tiled = lax.dot_general(
        jnp.dot(spread, mixing_ref[0], precision=lax.Precision.HIGHEST, preferred_element_type=F32),
        spread,
        (((1,), (1,)), ((), ())),
        precision=lax.Precision.HIGHEST,
        preferred_element_type=F32,
    )
    same = lax.div(lax.broadcasted_iota(I32, (ROWS, ROWS), 0), LEV) == lax.div(
        lax.broadcasted_iota(I32, (ROWS, ROWS), 1), LEV
    )
    mix_high, mix_low = halves(jnp.where(same, tiled, 0.0))
    mix_both = jnp.concatenate(
        [
            jnp.concatenate([mix_high, mix_high], axis=1),
            jnp.concatenate([mix_low, mix_low], axis=1),
        ],
        axis=0,
    )

    loads[3].wait()
    loads[4].wait()
    for halo in halos:
        halo.wait_recv()

    def split_block(e):
        cells = pl.ds(pl.multiple_of(e * LANES, LANES), LANES)
        for v in range(VARS):
            at = pl.ds(pl.multiple_of(e * ROWS + v * LEV, LEV), LEV)
            high, low = halves(ext[v, :, cells])
            split[at, 0:LANES] = high
            split[at, LANES : 2 * LANES] = low

    for e in range(SPAN - 1):
        split_block(e)

    def stencil(b, c_):
        base = pl.multiple_of(b * LANES, LANES)
        split_block(b + SPAN - 1)
        window = split[pl.ds(pl.multiple_of(b * ROWS, ROWS), SPAN * ROWS), :]
        near = nbr[:, pl.ds(base, LANES)]
        coefs = coef[:, pl.ds(base, LANES)]
        place = lane + near
        at, block = (place & (LANES - 1)), place >> 7
        rest = 1.0 - jnp.sum(coefs, axis=0, keepdims=True)
        acc = [
            rest * ext[r // 2, (r % 2) * 8 : (r % 2) * 8 + 8, pl.ds(HALO + base, LANES)]
            for r in range(ROWS // 8)
        ]
        for pair in range(NBR // 2):
            hot = jnp.concatenate(
                [
                    jnp.where(lane_rows == at[j : j + 1].astype(I16), one, nought)
                    for j in (2 * pair, 2 * pair + 1)
                ],
                axis=1,
            )
            rows = jnp.dot(
                window, jnp.concatenate([hot, hot], axis=0), preferred_element_type=F32
            )
            for half in range(2):
                j = 2 * pair + half
                factor = jnp.broadcast_to(coefs[j : j + 1], (8, LANES))
                which = jnp.broadcast_to(block[j : j + 1], (8, LANES))
                for r in range(ROWS // 8):
                    pick = rows[r * 8 : r * 8 + 8, half * LANES : (half + 1) * LANES]
                    for s in range(1, SPAN):
                        pick = jnp.where(
                            which == s,
                            rows[
                                s * ROWS + r * 8 : s * ROWS + r * 8 + 8,
                                half * LANES : (half + 1) * LANES,
                            ],
                            pick,
                        )
                    acc[r] = acc[r] + factor * pick
        high, low = halves(jnp.concatenate(acc, axis=0))
        forced[0:ROWS, pl.ds(base, LANES)] = high
        forced[ROWS : 2 * ROWS, pl.ds(base, LANES)] = low
        return c_

    lax.fori_loop(0, BLOCKS, stencil, 0, unroll=STU)

    def mix(i, c_):
        cells = pl.ds(pl.multiple_of(i * 4 * LANES, 4 * LANES), 4 * LANES)
        result = jnp.dot(mix_both, forced[:, cells], preferred_element_type=F32)
        result = result[0:ROWS] + result[ROWS : 2 * ROWS]
        for v in range(VARS):
            mixed[v, :, cells] = result[v * LEV : (v + 1) * LEV]
        return c_

    lax.fori_loop(0, BLOCKS // 4, mix, 0, unroll=2)
    store = pltpu.make_async_copy(mixed, mixed_hbm, out_sem)
    store.start()

    loads[5].wait()
    by_peer(raw_target, target)
    total[...] = jnp.zeros_like(total)

    def scatter(step, c_):
        p = peer_at(me, step, -1)
        from_peer(p).wait_recv()
        cells = target[pl.ds(pl.multiple_of(p * CHUNKS, CHUNKS), CHUNKS), :]
        low, high = (cells & (LANES - 1)), (cells >> 7)
        values, hots = [], []
        for c in range(CHUNKS):
            here = block_rows == high[c : c + 1].astype(I16)
            hots.append(jnp.where(lane_rows == low[c : c + 1].astype(I16), one, nought))
            parts = [halves(recvbuf[p, v * 8 + c : v * 8 + c + 1, :]) for v in range(VARS)]
            values.append(
                jnp.concatenate(
                    [jnp.where(here, parts[v][i], nought) for i in range(2) for v in range(VARS)],
                    axis=0,
                )
            )
        total[...] += lax.dot_general(
            jnp.concatenate(values, axis=1),
            jnp.concatenate(hots, axis=1),
            (((1,), (1,)), ((), ())),
            preferred_element_type=F32,
        )
        return c_

    lax.fori_loop(0, PEERS, scatter, 0, unroll=SU)

    for v in range(VARS):
        for b in range(BLOCKS):
            r = v * BLOCKS + b
            flux_ref[v : v + 1, b * LANES : (b + 1) * LANES] = (
                total[r : r + 1, :] + total[r + VARS * BLOCKS : r + VARS * BLOCKS + 1, :]
            )

    def sent(step, c_):
        to_peer(step).wait_send()
        return c_

    lax.fori_loop(0, PEERS, sent, 0)
    for halo in halos:
        halo.wait_send()
    store.wait()


def local(
    model_state,
    neighbours,
    stencil_coef,
    column_mixing_operator,
    remap_count,
    remap_source,
    remap_weight,
    remap_target,
):
    hbm = pl.BlockSpec(memory_space=pltpu.HBM)
    vmem = pl.BlockSpec(memory_space=pltpu.VMEM)
    smem = pl.BlockSpec(memory_space=pltpu.SMEM)
    mixed, flux = pl.pallas_call(
        kernel,
        out_shape=(
            jax.ShapeDtypeStruct((VARS, LEV, CELLS), F32),
            jax.ShapeDtypeStruct((VARS, CELLS), F32),
        ),
        in_specs=[hbm, hbm, hbm, vmem, smem, hbm, hbm, hbm],
        out_specs=(hbm, vmem),
        scratch_shapes=[
            pltpu.VMEM((VARS, LEV, CELLS + 2 * HALO), F32),
            pltpu.VMEM((NBR, CELLS), I32),
            pltpu.VMEM((NBR, CELLS), F32),
            pltpu.VMEM((PEERS, CAP), I32),
            pltpu.VMEM((PEERS, CAP), F32),
            pltpu.VMEM((PEERS, CAP), I32),
            pltpu.VMEM((PEERS * CHUNKS, LANES), I32),
            pltpu.VMEM((PEERS * CHUNKS, LANES), F32),
            pltpu.VMEM((PEERS * CHUNKS, LANES), I32),
            pltpu.VMEM((VARS * BLOCKS, LANES), F32),
            pltpu.VMEM((PEERS, VARS * CHUNKS, LANES), F32),
            pltpu.VMEM((PEERS, VARS * CHUNKS, LANES), F32),
            pltpu.VMEM(((BLOCKS + SPAN - 1) * ROWS, 2 * LANES), BF16),
            pltpu.VMEM((2 * ROWS, CELLS), BF16),
            pltpu.VMEM((VARS, LEV, CELLS), F32),
            pltpu.VMEM((2 * VARS * BLOCKS, LANES), F32),
            pltpu.SemaphoreType.DMA((6,)),
            pltpu.SemaphoreType.DMA((2,)),
            pltpu.SemaphoreType.DMA((2,)),
            pltpu.SemaphoreType.DMA((PEERS,)),
            pltpu.SemaphoreType.DMA((PEERS,)),
            pltpu.SemaphoreType.DMA,
        ],
        compiler_params=pltpu.CompilerParams(
            collective_id=0, has_side_effects=True, vmem_limit_bytes=60 << 20
        ),
        name="step",
    )(
        model_state,
        neighbours,
        stencil_coef,
        column_mixing_operator,
        remap_count,
        remap_source,
        remap_weight,
        remap_target,
    )
    updated = mixed + column_mixing_operator[0, :, 0][None, :, None] * flux[:, None, :]
    return updated[None], flux[None]


def solution(mesh):
    in_specs = (
        P("comp", None, None, "dom"),
        P("comp", None, "dom"),
        P("comp", None, "dom"),
        P("comp", None, None),
        P("comp", "dom", None),
        P("comp", "dom", None, None),
        P("comp", "dom", None, None),
        P("comp", "dom", None, None),
    )
    out_specs = (P("comp", None, None, "dom"), P("comp", None, "dom"))
    return jax.shard_map(local, mesh=mesh, in_specs=in_specs, out_specs=out_specs, check_vma=False)
```

```python
import itertools
import random

import jax
import jax.numpy as jnp
from jax import lax
from jax.experimental import pallas as pl
from jax.experimental.pallas import tpu as pltpu
from jax.sharding import PartitionSpec as P

MESH = pl.DeviceIdType.MESH
F32, BF16, I32, I16 = jnp.float32, jnp.bfloat16, jnp.int32, jnp.int16
LANES = 128
SIDE = 4
PEERS = SIDE**3
VARS, LEV, NBR = 4, 16, 8
CELLS = 4096
CAP = 1024
HALO = 256
BLOCKS = CELLS // LANES
CHUNKS = CAP // LANES
ROWS = VARS * LEV
SPAN = 2 * HALO // LANES + 1
BATCH = 16
STENCIL_UNROLL = 4
FROM_LEFT, FROM_RIGHT = 0, HALO + CELLS


def halves(x):
    high = x.astype(BF16)
    return high, (x - high.astype(F32)).astype(BF16)


def lane_pick(table, index):
    return jnp.take_along_axis(table, index, axis=1, mode="promise_in_bounds")


def sublane_pick(table, index):
    return jnp.take_along_axis(table, index, axis=0, mode="promise_in_bounds")


def displacements():
    moves = list(itertools.product((0, 1, 2, -1), repeat=3))
    random.Random(1).shuffle(moves)
    ordered = []
    for move in moves:
        for one in (move, tuple(-m if m != 2 else 2 for m in move)):
            if one not in ordered:
                ordered.append(one)
    ordered.sort(key=lambda move: -sum(abs(m) for m in move))
    return [tuple(m % SIDE for m in move) for move in ordered]


ORDER = displacements()


def peer_at(me, group, k, sign):
    place = 0
    for axis, unit in enumerate((16, 4, 1)):
        at = lax.rem(lax.div(me, unit), SIDE)
        move = 0
        for g in range(PEERS // BATCH):
            step = ORDER[g * BATCH + k][axis]
            if step:
                move = move + jnp.where(group == g, step, 0)
        place = place + unit * lax.rem(at + sign * move + SIDE, SIDE)
    return place


def kernel(
    state_hbm,
    neighbours_hbm,
    coef_hbm,
    mixing_ref,
    count_ref,
    source_hbm,
    weight_hbm,
    target_hbm,
    mixed_hbm,
    flux_ref,
    ext,
    nbr,
    coef,
    raw_source,
    raw_weight,
    raw_target,
    source,
    weight,
    target,
    table,
    sendbuf,
    recvbuf,
    split,
    forced,
    mixed,
    total,
    in_sems,
    halo_send_sems,
    halo_recv_sems,
    send_sems,
    recv_sems,
    out_sem,
):
    comp, me = lax.axis_index("comp"), lax.axis_index("dom")
    other = 1 - comp
    right, left = lax.rem(me + 1, PEERS), lax.rem(me + PEERS - 1, PEERS)

    loads = [
        pltpu.make_async_copy(src, dst, in_sems.at[i])
        for i, (src, dst) in enumerate(
            (
                (state_hbm.at[0], ext.at[:, :, pl.ds(HALO, CELLS)]),
                (source_hbm.at[0, 0], raw_source),
                (weight_hbm.at[0, 0], raw_weight),
                (neighbours_hbm.at[0], nbr),
                (coef_hbm.at[0], coef),
                (target_hbm.at[0, 0], raw_target),
            )
        )
    ]
    for load in loads:
        load.start()

    barrier = pltpu.get_barrier_semaphore()

    def greet(step, c):
        pl.semaphore_signal(barrier, inc=1, device_id=(other, step), device_id_type=MESH)
        return c

    lax.fori_loop(0, PEERS, greet, 0)
    for side in (left, right):
        pl.semaphore_signal(barrier, inc=1, device_id=(comp, side), device_id_type=MESH)

    loads[0].wait()
    for v in range(VARS):
        for b in range(BLOCKS):
            table[v * BLOCKS + b : v * BLOCKS + b + 1, :] = ext[
                v, 0:1, HALO + b * LANES : HALO + (b + 1) * LANES
            ]
    table_halves = jnp.concatenate(halves(table[...]), axis=1)

    loads[1].wait()
    loads[2].wait()

    def by_peer(raw, tidy):
        for g in range(PEERS // 8):
            for c in range(CHUNKS):
                tidy[pl.ds(g * 8 * CHUNKS + c, 8, stride=CHUNKS), :] = raw[
                    g * 8 : g * 8 + 8, c * LANES : (c + 1) * LANES
                ]

    by_peer(raw_source, source)
    by_peer(raw_weight, weight)

    pl.semaphore_wait(barrier, PEERS + 2)

    halos = [
        pltpu.make_async_remote_copy(
            src_ref=state_hbm.at[0, :, :, pl.ds(start, HALO)],
            dst_ref=ext.at[:, :, pl.ds(place, HALO)],
            send_sem=halo_send_sems.at[i],
            recv_sem=halo_recv_sems.at[i],
            device_id=(comp, side),
            device_id_type=MESH,
        )
        for i, (start, place, side) in enumerate(
            ((CELLS - HALO, FROM_LEFT, right), (0, FROM_RIGHT, left))
        )
    ]
    for halo in halos:
        halo.start()

    sublane = lax.broadcasted_iota(I32, (8, LANES), 0)
    lane = lax.broadcasted_iota(I32, (8, LANES), 1)
    slot = sublane * LANES + lane
    lane_rows = lax.broadcasted_iota(I32, (LANES, 1), 0).astype(I16)
    block_rows = lax.broadcasted_iota(I32, (BLOCKS, 1), 0).astype(I16)
    one, nought = BF16(1), BF16(0)

    def to_peer(q):
        return pltpu.make_async_remote_copy(
            src_ref=sendbuf.at[q],
            dst_ref=recvbuf.at[me],
            send_sem=send_sems.at[q],
            recv_sem=recv_sems.at[me],
            device_id=(other, q),
            device_id_type=MESH,
        )

    def from_peer(p):
        return pltpu.make_async_remote_copy(
            src_ref=sendbuf.at[p],
            dst_ref=recvbuf.at[p],
            send_sem=send_sems.at[p],
            recv_sem=recv_sems.at[p],
            device_id=(other, p),
            device_id_type=MESH,
        )

    def gather_one(q):
        cells = source[pl.ds(pl.multiple_of(q * CHUNKS, CHUNKS), CHUNKS), :]
        low, high = cells & (LANES - 1), cells >> 7
        used = jnp.where(
            slot < count_ref[0, 0, q],
            weight[pl.ds(pl.multiple_of(q * CHUNKS, CHUNKS), CHUNKS), :],
            0.0,
        )
        out = [jnp.zeros((8, LANES), F32) for _ in range(VARS)]
        for n in range(CHUNKS // 2):
            lows = jnp.concatenate([low[2 * n : 2 * n + 1], low[2 * n + 1 : 2 * n + 2]], axis=1)
            hot = jnp.where(lane_rows == lows.astype(I16), one, nought)
            rows = jnp.dot(
                table_halves,
                jnp.concatenate([hot, hot], axis=0),
                preferred_element_type=F32,
            )
            for half in range(2):
                c = 2 * n + half
                row = jnp.broadcast_to(high[c : c + 1], (8, LANES))
                within, group = row & 7, row >> 3
                for v in range(VARS):
                    picks = [
                        sublane_pick(
                            rows[
                                v * BLOCKS + t * 8 : v * BLOCKS + t * 8 + 8,
                                half * LANES : (half + 1) * LANES,
                            ],
                            within,
                        )
                        for t in range(BLOCKS // 8)
                    ]
                    pick = jnp.where(
                        group < 2,
                        jnp.where(group == 0, picks[0], picks[1]),
                        jnp.where(group == 2, picks[2], picks[3]),
                    )
                    out[v] = jnp.where(sublane == c, pick, out[v])
        for v in range(VARS):
            sendbuf[q, v * 8 : v * 8 + 8, :] = out[v] * used

    def gather(group, c_):
        peers = [peer_at(me, group, k, 1) for k in range(BATCH)]
        for q in peers:
            gather_one(q)
        for q in peers:
            to_peer(q).start()
        return c_

    lax.fori_loop(0, PEERS // BATCH, gather, 0)

    spread = (
        lax.rem(lax.broadcasted_iota(I32, (ROWS, LEV), 0), LEV)
        == lax.broadcasted_iota(I32, (ROWS, LEV), 1)
    ).astype(F32)
    tiled = lax.dot_general(
        jnp.dot(spread, mixing_ref[0], precision=lax.Precision.HIGHEST, preferred_element_type=F32),
        spread,
        (((1,), (1,)), ((), ())),
        precision=lax.Precision.HIGHEST,
        preferred_element_type=F32,
    )
    same = lax.div(lax.broadcasted_iota(I32, (ROWS, ROWS), 0), LEV) == lax.div(
        lax.broadcasted_iota(I32, (ROWS, ROWS), 1), LEV
    )
    mix_high, mix_low = halves(jnp.where(same, tiled, 0.0))
    mix_both = jnp.concatenate(
        [
            jnp.concatenate([mix_high, mix_high], axis=1),
            jnp.concatenate([mix_low, mix_low], axis=1),
        ],
        axis=0,
    )

    loads[3].wait()
    loads[4].wait()
    for halo in halos:
        halo.wait_recv()

    def split_block(e):
        cells = pl.ds(pl.multiple_of(e * LANES, LANES), LANES)
        for v in range(VARS):
            at = pl.ds(pl.multiple_of(e * ROWS + v * LEV, LEV), LEV)
            high, low = halves(ext[v, :, cells])
            split[at, 0:LANES] = high
            split[at, LANES : 2 * LANES] = low

    for e in range(SPAN - 1):
        split_block(e)

    def stencil(b, c_):
        base = pl.multiple_of(b * LANES, LANES)
        split_block(b + SPAN - 1)
        window = split[pl.ds(pl.multiple_of(b * ROWS, ROWS), SPAN * ROWS), :]
        near = nbr[:, pl.ds(base, LANES)]
        coefs = coef[:, pl.ds(base, LANES)]
        place = lane + near
        at, block = (place & (LANES - 1)), place >> 7
        rest = 1.0 - jnp.sum(coefs, axis=0, keepdims=True)
        acc = [
            rest * ext[r // 2, (r % 2) * 8 : (r % 2) * 8 + 8, pl.ds(HALO + base, LANES)]
            for r in range(ROWS // 8)
        ]
        for pair in range(NBR // 2):
            hot = jnp.concatenate(
                [
                    jnp.where(lane_rows == at[j : j + 1].astype(I16), one, nought)
                    for j in (2 * pair, 2 * pair + 1)
                ],
                axis=1,
            )
            rows = jnp.dot(
                window, jnp.concatenate([hot, hot], axis=0), preferred_element_type=F32
            )
            for half in range(2):
                j = 2 * pair + half
                factor = jnp.broadcast_to(coefs[j : j + 1], (8, LANES))
                which = jnp.broadcast_to(block[j : j + 1], (8, LANES))
                for r in range(ROWS // 8):
                    pick = rows[r * 8 : r * 8 + 8, half * LANES : (half + 1) * LANES]
                    for s in range(1, SPAN):
                        pick = jnp.where(
                            which == s,
                            rows[
                                s * ROWS + r * 8 : s * ROWS + r * 8 + 8,
                                half * LANES : (half + 1) * LANES,
                            ],
                            pick,
                        )
                    acc[r] = acc[r] + factor * pick
        high, low = halves(jnp.concatenate(acc, axis=0))
        forced[0:ROWS, pl.ds(base, LANES)] = high
        forced[ROWS : 2 * ROWS, pl.ds(base, LANES)] = low
        return c_

    lax.fori_loop(0, BLOCKS, stencil, 0, unroll=STENCIL_UNROLL)

    def mix(i, c_):
        cells = pl.ds(pl.multiple_of(i * 4 * LANES, 4 * LANES), 4 * LANES)
        result = jnp.dot(mix_both, forced[:, cells], preferred_element_type=F32)
        result = result[0:ROWS] + result[ROWS : 2 * ROWS]
        for v in range(VARS):
            mixed[v, :, cells] = result[v * LEV : (v + 1) * LEV]
        return c_

    lax.fori_loop(0, BLOCKS // 4, mix, 0, unroll=2)
    store = pltpu.make_async_copy(mixed, mixed_hbm, out_sem)
    store.start()

    loads[5].wait()
    by_peer(raw_target, target)
    total[...] = jnp.zeros_like(total)

    def scatter_one(p):
        cells = target[pl.ds(pl.multiple_of(p * CHUNKS, CHUNKS), CHUNKS), :]
        low, high = (cells & (LANES - 1)), (cells >> 7)
        values, hots = [], []
        for c in range(CHUNKS):
            here = block_rows == high[c : c + 1].astype(I16)
            hots.append(jnp.where(lane_rows == low[c : c + 1].astype(I16), one, nought))
            parts = [halves(recvbuf[p, v * 8 + c : v * 8 + c + 1, :]) for v in range(VARS)]
            values.append(
                jnp.concatenate(
                    [jnp.where(here, parts[v][i], nought) for i in range(2) for v in range(VARS)],
                    axis=0,
                )
            )
        total[...] += lax.dot_general(
            jnp.concatenate(values, axis=1),
            jnp.concatenate(hots, axis=1),
            (((1,), (1,)), ((), ())),
            preferred_element_type=F32,
        )

    def scatter(group, c_):
        peers = [peer_at(me, group, k, -1) for k in range(BATCH)]
        for p in peers:
            from_peer(p).wait_recv()
        for p in peers:
            scatter_one(p)
        return c_

    lax.fori_loop(0, PEERS // BATCH, scatter, 0)

    for v in range(VARS):
        for b in range(BLOCKS):
            r = v * BLOCKS + b
            flux_ref[v : v + 1, b * LANES : (b + 1) * LANES] = (
                total[r : r + 1, :] + total[r + VARS * BLOCKS : r + VARS * BLOCKS + 1, :]
            )

    def sent(step, c_):
        to_peer(step).wait_send()
        return c_

    lax.fori_loop(0, PEERS, sent, 0)
    for halo in halos:
        halo.wait_send()
    store.wait()


def finish(
    mixed_hbm, flux_ref, mixing_ref, updated_hbm, flux_hbm, state, load_sems, store_sems, flux_sem
):
    loads = [
        pltpu.make_async_copy(mixed_hbm.at[v], state.at[v], load_sems.at[v]) for v in range(VARS)
    ]
    for load in loads:
        load.start()
    flux_store = pltpu.make_async_copy(flux_ref, flux_hbm.at[0], flux_sem)
    flux_store.start()
    stores = []
    shares = [
        jnp.broadcast_to(mixing_ref[0, h * 8 : h * 8 + 8, 0:1], (8, LANES)) for h in range(LEV // 8)
    ]
    for v in range(VARS):
        loads[v].wait()
        for b in range(BLOCKS):
            cells = slice(b * LANES, (b + 1) * LANES)
            row = jnp.broadcast_to(flux_ref[v : v + 1, cells], (8, LANES))
            for h in range(LEV // 8):
                levels = slice(h * 8, h * 8 + 8)
                state[v, levels, cells] = state[v, levels, cells] + shares[h] * row
        store = pltpu.make_async_copy(state.at[v], updated_hbm.at[0, v], store_sems.at[v])
        store.start()
        stores.append(store)
    for store in stores:
        store.wait()
    flux_store.wait()


def local(
    model_state,
    neighbours,
    stencil_coef,
    column_mixing_operator,
    remap_count,
    remap_source,
    remap_weight,
    remap_target,
):
    hbm = pl.BlockSpec(memory_space=pltpu.HBM)
    vmem = pl.BlockSpec(memory_space=pltpu.VMEM)
    smem = pl.BlockSpec(memory_space=pltpu.SMEM)
    mixed, flux = pl.pallas_call(
        kernel,
        out_shape=(
            jax.ShapeDtypeStruct((VARS, LEV, CELLS), F32),
            jax.ShapeDtypeStruct((VARS, CELLS), F32),
        ),
        in_specs=[hbm, hbm, hbm, vmem, smem, hbm, hbm, hbm],
        out_specs=(hbm, vmem),
        scratch_shapes=[
            pltpu.VMEM((VARS, LEV, CELLS + 2 * HALO), F32),
            pltpu.VMEM((NBR, CELLS), I32),
            pltpu.VMEM((NBR, CELLS), F32),
            pltpu.VMEM((PEERS, CAP), I32),
            pltpu.VMEM((PEERS, CAP), F32),
            pltpu.VMEM((PEERS, CAP), I32),
            pltpu.VMEM((PEERS * CHUNKS, LANES), I32),
            pltpu.VMEM((PEERS * CHUNKS, LANES), F32),
            pltpu.VMEM((PEERS * CHUNKS, LANES), I32),
            pltpu.VMEM((VARS * BLOCKS, LANES), F32),
            pltpu.VMEM((PEERS, VARS * CHUNKS, LANES), F32),
            pltpu.VMEM((PEERS, VARS * CHUNKS, LANES), F32),
            pltpu.VMEM(((BLOCKS + SPAN - 1) * ROWS, 2 * LANES), BF16),
            pltpu.VMEM((2 * ROWS, CELLS), BF16),
            pltpu.VMEM((VARS, LEV, CELLS), F32),
            pltpu.VMEM((2 * VARS * BLOCKS, LANES), F32),
            pltpu.SemaphoreType.DMA((6,)),
            pltpu.SemaphoreType.DMA((2,)),
            pltpu.SemaphoreType.DMA((2,)),
            pltpu.SemaphoreType.DMA((PEERS,)),
            pltpu.SemaphoreType.DMA((PEERS,)),
            pltpu.SemaphoreType.DMA,
        ],
        compiler_params=pltpu.CompilerParams(
            collective_id=0, has_side_effects=True, vmem_limit_bytes=60 << 20
        ),
        name="step",
    )(
        model_state,
        neighbours,
        stencil_coef,
        column_mixing_operator,
        remap_count,
        remap_source,
        remap_weight,
        remap_target,
    )
    return pl.pallas_call(
        finish,
        out_shape=(
            jax.ShapeDtypeStruct((1, VARS, LEV, CELLS), F32),
            jax.ShapeDtypeStruct((1, VARS, CELLS), F32),
        ),
        in_specs=[hbm, vmem, vmem],
        out_specs=(hbm, hbm),
        scratch_shapes=[
            pltpu.VMEM((VARS, LEV, CELLS), F32),
            pltpu.SemaphoreType.DMA((VARS,)),
            pltpu.SemaphoreType.DMA((VARS,)),
            pltpu.SemaphoreType.DMA,
        ],
        compiler_params=pltpu.CompilerParams(vmem_limit_bytes=60 << 20),
        name="finish",
    )(mixed, flux, column_mixing_operator)


def solution(mesh):
    in_specs = (
        P("comp", None, None, "dom"),
        P("comp", None, "dom"),
        P("comp", None, "dom"),
        P("comp", None, None),
        P("comp", "dom", None),
        P("comp", "dom", None, None),
        P("comp", "dom", None, None),
        P("comp", "dom", None, None),
    )
    out_specs = (P("comp", None, None, "dom"), P("comp", None, "dom"))
    return jax.shard_map(local, mesh=mesh, in_specs=in_specs, out_specs=out_specs, check_vma=False)
```

```python
import itertools
import random

import jax
import jax.numpy as jnp
from jax import lax
from jax.experimental import pallas as pl
from jax.experimental.pallas import tpu as pltpu
from jax.sharding import PartitionSpec as P

MESH = pl.DeviceIdType.MESH
F32, BF16, I32, I16 = jnp.float32, jnp.bfloat16, jnp.int32, jnp.int16
LANES = 128
SIDE = 4
PEERS = SIDE**3
VARS, LEV, NBR = 4, 16, 8
CELLS = 4096
CAP = 1024
HALO = 256
BLOCKS = CELLS // LANES
CHUNKS = CAP // LANES
ROWS = VARS * LEV
SPAN = 2 * HALO // LANES + 1
BATCH = 16
STENCIL_UNROLL = 4
PRODUCTS = 4
FROM_LEFT, FROM_RIGHT = 0, HALO + CELLS


def halves(x):
    high = x.astype(BF16)
    return high, (x - high.astype(F32)).astype(BF16)


def lane_pick(table, index):
    return jnp.take_along_axis(table, index, axis=1, mode="promise_in_bounds")


def sublane_pick(table, index):
    return jnp.take_along_axis(table, index, axis=0, mode="promise_in_bounds")


def displacements():
    moves = list(itertools.product((0, 1, 2, -1), repeat=3))
    random.Random(1).shuffle(moves)
    ordered = []
    for move in moves:
        for one in (move, tuple(-m if m != 2 else 2 for m in move)):
            if one not in ordered:
                ordered.append(one)
    ordered.sort(key=lambda move: -sum(abs(m) for m in move))
    return [tuple(m % SIDE for m in move) for move in ordered]


ORDER = displacements()


def peer_at(me, group, k, sign):
    place = 0
    for axis, unit in enumerate((16, 4, 1)):
        at = lax.rem(lax.div(me, unit), SIDE)
        move = 0
        for g in range(PEERS // BATCH):
            step = ORDER[g * BATCH + k][axis]
            if step:
                move = move + jnp.where(group == g, step, 0)
        place = place + unit * lax.rem(at + sign * move + SIDE, SIDE)
    return place


def kernel(
    state_hbm,
    neighbours_hbm,
    coef_hbm,
    mixing_hbm,
    count_hbm,
    source_hbm,
    weight_hbm,
    target_hbm,
    mixed_hbm,
    flux_hbm,
    ext,
    blended,
    mixing,
    count,
    flux,
    nbr,
    coef,
    raw_source,
    raw_weight,
    raw_target,
    source,
    weight,
    target,
    table,
    sendbuf,
    recvbuf,
    split,
    mixed,
    total,
    in_sems,
    halo_send_sems,
    halo_recv_sems,
    send_sems,
    recv_sems,
    out_sems,
    flux_sem,
):
    comp, me = lax.axis_index("comp"), lax.axis_index("dom")
    other = 1 - comp
    right, left = lax.rem(me + 1, PEERS), lax.rem(me + PEERS - 1, PEERS)

    def load(i, src, dst):
        return pltpu.make_async_copy(src, dst, in_sems.at[i])

    inner = pl.ds(HALO, CELLS)
    state_loads = [
        load(h, state_hbm.at[0, :, pl.ds(8 * h, 8), :], ext.at[:, pl.ds(8 * h, 8), inner])
        for h in range(2)
    ]
    source_load = load(2, source_hbm.at[0, 0], raw_source)
    weight_load = load(3, weight_hbm.at[0, 0], raw_weight)
    count_load = load(4, count_hbm.at[0], count)
    early = [state_loads[0], source_load, weight_load, count_load]
    mixing_load = load(5, mixing_hbm.at[0], mixing)
    target_load = load(6, target_hbm.at[0, 0], raw_target)
    stencil_loads = [load(7, neighbours_hbm.at[0], nbr), load(8, coef_hbm.at[0], coef)]
    late = [state_loads[1], mixing_load, *stencil_loads, target_load]
    for one_load in early + late:
        one_load.start()

    barrier = pltpu.get_barrier_semaphore()

    def greet(step, c):
        pl.semaphore_signal(barrier, inc=1, device_id=(other, step), device_id_type=MESH)
        return c

    lax.fori_loop(0, PEERS, greet, 0)
    for side in (left, right):
        pl.semaphore_signal(barrier, inc=1, device_id=(comp, side), device_id_type=MESH)

    state_loads[0].wait()
    for v in range(VARS):
        for b in range(BLOCKS):
            table[v * BLOCKS + b : v * BLOCKS + b + 1, :] = ext[
                v, 0:1, HALO + b * LANES : HALO + (b + 1) * LANES
            ]
    table_halves = jnp.concatenate(halves(table[...]), axis=1)

    source_load.wait()
    weight_load.wait()
    count_load.wait()

    def by_peer(raw, tidy):
        for g in range(PEERS // 8):
            for c in range(CHUNKS):
                tidy[pl.ds(g * 8 * CHUNKS + c, 8, stride=CHUNKS), :] = raw[
                    g * 8 : g * 8 + 8, c * LANES : (c + 1) * LANES
                ]

    by_peer(raw_source, source)
    by_peer(raw_weight, weight)

    halos = [
        pltpu.make_async_remote_copy(
            src_ref=state_hbm.at[0, :, :, pl.ds(start, HALO)],
            dst_ref=ext.at[:, :, pl.ds(place, HALO)],
            send_sem=halo_send_sems.at[i],
            recv_sem=halo_recv_sems.at[i],
            device_id=(comp, side),
            device_id_type=MESH,
        )
        for i, (start, place, side) in enumerate(
            ((CELLS - HALO, FROM_LEFT, right), (0, FROM_RIGHT, left))
        )
    ]

    sublane = lax.broadcasted_iota(I32, (8, LANES), 0)
    lane = lax.broadcasted_iota(I32, (8, LANES), 1)
    slot = sublane * LANES + lane
    lane_rows = lax.broadcasted_iota(I32, (LANES, 1), 0).astype(I16)
    block_rows = lax.broadcasted_iota(I32, (BLOCKS, 1), 0).astype(I16)
    one, nought = BF16(1), BF16(0)

    def to_peer(q):
        return pltpu.make_async_remote_copy(
            src_ref=sendbuf.at[q],
            dst_ref=recvbuf.at[me],
            send_sem=send_sems.at[q],
            recv_sem=recv_sems.at[me],
            device_id=(other, q),
            device_id_type=MESH,
        )

    def from_peer(p):
        return pltpu.make_async_remote_copy(
            src_ref=sendbuf.at[p],
            dst_ref=recvbuf.at[p],
            send_sem=send_sems.at[p],
            recv_sem=recv_sems.at[p],
            device_id=(other, p),
            device_id_type=MESH,
        )

    def gather_one(q):
        cells = source[pl.ds(pl.multiple_of(q * CHUNKS, CHUNKS), CHUNKS), :]
        low, high = cells & (LANES - 1), cells >> 7
        used = jnp.where(
            slot < count[0, q],
            weight[pl.ds(pl.multiple_of(q * CHUNKS, CHUNKS), CHUNKS), :],
            0.0,
        )
        out = [jnp.zeros((8, LANES), F32) for _ in range(VARS)]
        for n in range(CHUNKS // 2):
            lows = jnp.concatenate([low[2 * n : 2 * n + 1], low[2 * n + 1 : 2 * n + 2]], axis=1)
            hot = jnp.where(lane_rows == lows.astype(I16), one, nought)
            rows = jnp.dot(
                table_halves,
                jnp.concatenate([hot, hot], axis=0),
                preferred_element_type=F32,
            )
            for half in range(2):
                c = 2 * n + half
                row = jnp.broadcast_to(high[c : c + 1], (8, LANES))
                within, group = row & 7, row >> 3
                for v in range(VARS):
                    picks = [
                        sublane_pick(
                            rows[
                                v * BLOCKS + t * 8 : v * BLOCKS + t * 8 + 8,
                                half * LANES : (half + 1) * LANES,
                            ],
                            within,
                        )
                        for t in range(BLOCKS // 8)
                    ]
                    pick = jnp.where(
                        group < 2,
                        jnp.where(group == 0, picks[0], picks[1]),
                        jnp.where(group == 2, picks[2], picks[3]),
                    )
                    out[v] = jnp.where(sublane == c, pick, out[v])
        for v in range(VARS):
            sendbuf[q, v * 8 : v * 8 + 8, :] = out[v] * used

    def gather(group, c_):
        peers = [peer_at(me, group, k, 1) for k in range(BATCH)]
        for q in peers:
            gather_one(q)

        @pl.when(group == 0)
        def _():
            pl.semaphore_wait(barrier, PEERS + 2)
            for halo in halos:
                halo.start()

        for q in peers:
            to_peer(q).start()
        return c_

    lax.fori_loop(0, PEERS // BATCH, gather, 0)

    mixing_load.wait()
    spread = (
        lax.rem(lax.broadcasted_iota(I32, (ROWS, LEV), 0), LEV)
        == lax.broadcasted_iota(I32, (ROWS, LEV), 1)
    ).astype(F32)
    tiled = lax.dot_general(
        jnp.dot(spread, mixing[...], precision=lax.Precision.HIGHEST, preferred_element_type=F32),
        spread,
        (((1,), (1,)), ((), ())),
        precision=lax.Precision.HIGHEST,
        preferred_element_type=F32,
    )
    same = lax.div(lax.broadcasted_iota(I32, (ROWS, ROWS), 0), LEV) == lax.div(
        lax.broadcasted_iota(I32, (ROWS, ROWS), 1), LEV
    )
    mix_high, mix_low = halves(jnp.where(same, tiled, 0.0))
    mix_both = jnp.concatenate(
        [
            jnp.concatenate([mix_high, mix_high], axis=1),
            jnp.concatenate([mix_low, mix_low], axis=1),
        ],
        axis=0,
    )

    state_loads[1].wait()
    for halo in halos:
        halo.wait_recv()

    def blend(i, c_):
        cells = pl.ds(pl.multiple_of(i * 4 * LANES, 4 * LANES), 4 * LANES)
        both = jnp.concatenate(
            [halves(ext[v, :, cells])[part] for part in range(2) for v in range(VARS)], axis=0
        )
        result = jnp.dot(mix_both, both, preferred_element_type=F32)
        result = result[0:ROWS] + result[ROWS : 2 * ROWS]
        for v in range(VARS):
            blended[v, :, cells] = result[v * LEV : (v + 1) * LEV]
        high, low = halves(result)
        for e in range(4):
            at = pl.ds(pl.multiple_of((i * 4 + e) * ROWS, ROWS), ROWS)
            split[at, 0:LANES] = high[:, e * LANES : (e + 1) * LANES]
            split[at, LANES : 2 * LANES] = low[:, e * LANES : (e + 1) * LANES]
        return c_

    lax.fori_loop(0, (BLOCKS + SPAN - 1) // 4, blend, 0, unroll=3)
    for one_load in stencil_loads:
        one_load.wait()

    def rows_at(r, cells):
        return blended[r // 2, (r % 2) * 8 : (r % 2) * 8 + 8, cells]

    def stencil(b, c_):
        base = pl.multiple_of(b * LANES, LANES)
        window = split[pl.ds(pl.multiple_of(b * ROWS, ROWS), SPAN * ROWS), :]
        coefs = coef[:, pl.ds(base, LANES)]
        place = lane + nbr[:, pl.ds(base, LANES)]
        at, block = (place & (LANES - 1)), place >> 7
        rest = 1.0 - jnp.sum(coefs, axis=0, keepdims=True)
        acc = [rest * rows_at(r, pl.ds(HALO + base, LANES)) for r in range(ROWS // 8)]
        for pair in range(PRODUCTS // 2):
            hot = jnp.concatenate(
                [
                    jnp.where(lane_rows == at[j : j + 1].astype(I16), one, nought)
                    for j in (2 * pair, 2 * pair + 1)
                ],
                axis=1,
            )
            rows = jnp.dot(
                window, jnp.concatenate([hot, hot], axis=0), preferred_element_type=F32
            )
            for half in range(2):
                j = 2 * pair + half
                factor = jnp.broadcast_to(coefs[j : j + 1], (8, LANES))
                which = jnp.broadcast_to(block[j : j + 1], (8, LANES))
                lanes = slice(half * LANES, (half + 1) * LANES)
                for r in range(ROWS // 8):
                    pick = rows[r * 8 : r * 8 + 8, lanes]
                    for s in range(1, SPAN):
                        row = s * ROWS + r * 8
                        pick = jnp.where(which == s, rows[row : row + 8, lanes], pick)
                    acc[r] = acc[r] + factor * pick
        for r in range(ROWS // 8):
            mixed[r // 2, (r % 2) * 8 : (r % 2) * 8 + 8, pl.ds(base, LANES)] = acc[r]
        return c_

    lax.fori_loop(0, BLOCKS, stencil, 0, unroll=STENCIL_UNROLL)

    def permuted(b, rows):
        base = pl.multiple_of(b * LANES, LANES)
        cells = pl.ds(base, LANES)
        coefs = coef[:, cells]
        place = lane + nbr[:, cells]
        at, block = (place & (LANES - 1)), place >> 7
        acc = [mixed[r // 2, (r % 2) * 8 : (r % 2) * 8 + 8, cells] for r in rows]
        for j in range(PRODUCTS, NBR):
            turn = jnp.broadcast_to(at[j : j + 1], (8, LANES))
            which = jnp.broadcast_to(block[j : j + 1], (8, LANES))
            factor = jnp.broadcast_to(coefs[j : j + 1], (8, LANES))
            for i, r in enumerate(rows):
                pick = lane_pick(rows_at(r, cells), turn)
                for s in range(1, SPAN):
                    other_pick = lane_pick(rows_at(r, pl.ds(base + s * LANES, LANES)), turn)
                    pick = jnp.where(which == s, other_pick, pick)
                acc[i] = acc[i] + factor * pick
        for i, r in enumerate(rows):
            mixed[r // 2, (r % 2) * 8 : (r % 2) * 8 + 8, cells] = acc[i]

    target_load.wait()
    by_peer(raw_target, target)
    total[...] = jnp.zeros_like(total)

    def scatter_one(p):
        cells = target[pl.ds(pl.multiple_of(p * CHUNKS, CHUNKS), CHUNKS), :]
        low, high = (cells & (LANES - 1)), (cells >> 7)
        values, hots = [], []
        for c in range(CHUNKS):
            here = block_rows == high[c : c + 1].astype(I16)
            hots.append(jnp.where(lane_rows == low[c : c + 1].astype(I16), one, nought))
            parts = [halves(recvbuf[p, v * 8 + c : v * 8 + c + 1, :]) for v in range(VARS)]
            values.append(
                jnp.concatenate(
                    [jnp.where(here, parts[v][i], nought) for i in range(2) for v in range(VARS)],
                    axis=0,
                )
            )
        total[...] += lax.dot_general(
            jnp.concatenate(values, axis=1),
            jnp.concatenate(hots, axis=1),
            (((1,), (1,)), ((), ())),
            preferred_element_type=F32,
        )

    def store_of(group):
        width = CELLS * BATCH // PEERS
        cells = pl.ds(pl.multiple_of(group * width, width), width)
        return pltpu.make_async_copy(
            mixed.at[:, :, cells], mixed_hbm.at[:, :, cells], out_sems.at[group]
        )

    def scatter(group, c_):
        peers = [peer_at(me, group, k, -1) for k in range(BATCH)]
        for p in peers:
            from_peer(p).wait_recv()
        for k, p in enumerate(peers):
            scatter_one(p)
            half = ROWS // 16
            permuted(group * (BATCH // 2) + k // 2, range(k % 2 * half, (k % 2 + 1) * half))
        store_of(group).start()
        return c_

    lax.fori_loop(0, PEERS // BATCH, scatter, 0)

    for v in range(VARS):
        for b in range(BLOCKS):
            r = v * BLOCKS + b
            flux[v : v + 1, b * LANES : (b + 1) * LANES] = (
                total[r : r + 1, :] + total[r + VARS * BLOCKS : r + VARS * BLOCKS + 1, :]
            )

    flux_store = pltpu.make_async_copy(flux, flux_hbm, flux_sem)
    flux_store.start()

    def sent(step, c_):
        to_peer(step).wait_send()
        return c_

    lax.fori_loop(0, PEERS, sent, 0)
    for halo in halos:
        halo.wait_send()
    for group in range(PEERS // BATCH):
        store_of(group).wait()
    flux_store.wait()


def finish(
    mixed_hbm, flux_in, mixing_hbm, updated_hbm, flux_out, state, flux, mixing, load_sems, store_sems
):
    loads = [
        pltpu.make_async_copy(mixed_hbm.at[v], state.at[v], load_sems.at[v]) for v in range(VARS)
    ]
    flux_load = pltpu.make_async_copy(flux_in, flux, load_sems.at[VARS])
    mixing_load = pltpu.make_async_copy(mixing_hbm.at[0], mixing, load_sems.at[VARS + 1])
    for load in [flux_load, mixing_load, *loads]:
        load.start()
    flux_load.wait()
    mixing_load.wait()
    flux_store = pltpu.make_async_copy(flux, flux_out.at[0], store_sems.at[VARS])
    flux_store.start()
    stores = []
    shares = [
        jnp.broadcast_to(mixing[h * 8 : h * 8 + 8, 0:1], (8, LANES)) for h in range(LEV // 8)
    ]
    for v in range(VARS):
        loads[v].wait()
        for b in range(BLOCKS):
            cells = slice(b * LANES, (b + 1) * LANES)
            row = jnp.broadcast_to(flux[v : v + 1, cells], (8, LANES))
            for h in range(LEV // 8):
                levels = slice(h * 8, h * 8 + 8)
                state[v, levels, cells] = state[v, levels, cells] + shares[h] * row
        store = pltpu.make_async_copy(state.at[v], updated_hbm.at[0, v], store_sems.at[v])
        store.start()
        stores.append(store)
    for store in stores:
        store.wait()
    flux_store.wait()


def local(
    model_state,
    neighbours,
    stencil_coef,
    column_mixing_operator,
    remap_count,
    remap_source,
    remap_weight,
    remap_target,
):
    hbm = pl.BlockSpec(memory_space=pltpu.HBM)
    mixed, flux = pl.pallas_call(
        kernel,
        out_shape=(
            jax.ShapeDtypeStruct((VARS, LEV, CELLS), F32),
            jax.ShapeDtypeStruct((VARS, CELLS), F32),
        ),
        in_specs=[hbm] * 8,
        out_specs=(hbm, hbm),
        scratch_shapes=[
            pltpu.VMEM((VARS, LEV, CELLS + 2 * HALO), F32),
            pltpu.VMEM((VARS, LEV, CELLS + 2 * HALO), F32),
            pltpu.VMEM((LEV, LEV), F32),
            pltpu.SMEM((1, PEERS), I32),
            pltpu.VMEM((VARS, CELLS), F32),
            pltpu.VMEM((NBR, CELLS), I32),
            pltpu.VMEM((NBR, CELLS), F32),
            pltpu.VMEM((PEERS, CAP), I32),
            pltpu.VMEM((PEERS, CAP), F32),
            pltpu.VMEM((PEERS, CAP), I32),
            pltpu.VMEM((PEERS * CHUNKS, LANES), I32),
            pltpu.VMEM((PEERS * CHUNKS, LANES), F32),
            pltpu.VMEM((PEERS * CHUNKS, LANES), I32),
            pltpu.VMEM((VARS * BLOCKS, LANES), F32),
            pltpu.VMEM((PEERS, VARS * CHUNKS, LANES), F32),
            pltpu.VMEM((PEERS, VARS * CHUNKS, LANES), F32),
            pltpu.VMEM(((BLOCKS + SPAN - 1) * ROWS, 2 * LANES), BF16),
            pltpu.VMEM((VARS, LEV, CELLS), F32),
            pltpu.VMEM((2 * VARS * BLOCKS, LANES), F32),
            pltpu.SemaphoreType.DMA((9,)),
            pltpu.SemaphoreType.DMA((2,)),
            pltpu.SemaphoreType.DMA((2,)),
            pltpu.SemaphoreType.DMA((PEERS,)),
            pltpu.SemaphoreType.DMA((PEERS,)),
            pltpu.SemaphoreType.DMA((PEERS // BATCH,)),
            pltpu.SemaphoreType.DMA,
        ],
        compiler_params=pltpu.CompilerParams(
            collective_id=0, has_side_effects=True, vmem_limit_bytes=60 << 20
        ),
        name="step",
    )(
        model_state,
        neighbours,
        stencil_coef,
        column_mixing_operator,
        remap_count,
        remap_source,
        remap_weight,
        remap_target,
    )
    return pl.pallas_call(
        finish,
        out_shape=(
            jax.ShapeDtypeStruct((1, VARS, LEV, CELLS), F32),
            jax.ShapeDtypeStruct((1, VARS, CELLS), F32),
        ),
        in_specs=[hbm] * 3,
        out_specs=(hbm, hbm),
        scratch_shapes=[
            pltpu.VMEM((VARS, LEV, CELLS), F32),
            pltpu.VMEM((VARS, CELLS), F32),
            pltpu.VMEM((LEV, LEV), F32),
            pltpu.SemaphoreType.DMA((VARS + 2,)),
            pltpu.SemaphoreType.DMA((VARS + 1,)),
        ],
        compiler_params=pltpu.CompilerParams(vmem_limit_bytes=60 << 20),
        name="finish",
    )(mixed, flux, column_mixing_operator)


def solution(mesh):
    in_specs = (
        P("comp", None, None, "dom"),
        P("comp", None, "dom"),
        P("comp", None, "dom"),
        P("comp", None, None),
        P("comp", "dom", None),
        P("comp", "dom", None, None),
        P("comp", "dom", None, None),
        P("comp", "dom", None, None),
    )
    out_specs = (P("comp", None, None, "dom"), P("comp", None, "dom"))
    return jax.shard_map(local, mesh=mesh, in_specs=in_specs, out_specs=out_specs, check_vma=False)
```

```python
import itertools
import random

import jax
import jax.numpy as jnp
from jax import lax
from jax.experimental import pallas as pl
from jax.experimental.pallas import tpu as pltpu
from jax.sharding import PartitionSpec as P

MESH = pl.DeviceIdType.MESH
F32, BF16, I32, I16 = jnp.float32, jnp.bfloat16, jnp.int32, jnp.int16
LANES = 128
SIDE = 4
PEERS = SIDE**3
VARS, LEV, NBR = 4, 16, 8
CELLS = 4096
CAP = 1024
HALO = 256
BLOCKS = CELLS // LANES
CHUNKS = CAP // LANES
ROWS = VARS * LEV
SPAN = 2 * HALO // LANES + 1
BATCH = 16
STENCIL_UNROLL = 4
PRODUCTS = 4
FROM_LEFT, FROM_RIGHT = 0, HALO + CELLS


def halves(x):
    high = x.astype(BF16)
    return high, (x - high.astype(F32)).astype(BF16)


def lane_pick(table, index):
    return jnp.take_along_axis(table, index, axis=1, mode="promise_in_bounds")


def sublane_pick(table, index):
    return jnp.take_along_axis(table, index, axis=0, mode="promise_in_bounds")


def displacements():
    moves = list(itertools.product((0, 1, 2, -1), repeat=3))
    random.Random(1).shuffle(moves)
    ordered = []
    for move in moves:
        for one in (move, tuple(-m if m != 2 else 2 for m in move)):
            if one not in ordered:
                ordered.append(one)
    ordered.sort(key=lambda move: sum(abs(m) for m in move))
    return [tuple(m % SIDE for m in move) for move in ordered]


ORDER = displacements()


def places(me, sign):
    return [
        [
            unit * lax.rem(lax.rem(lax.div(me, unit), SIDE) + sign * move + SIDE, SIDE)
            for move in range(SIDE)
        ]
        for unit in (SIDE * SIDE, SIDE, 1)
    ]


def peer_at(places_, group, k):
    place = 0
    for g in range(PEERS // BATCH):
        there = sum(places_[axis][move] for axis, move in enumerate(ORDER[g * BATCH + k]))
        place = there if g == 0 else jnp.where(group == g, there, place)
    return place


def kernel(
    state_hbm,
    neighbours_hbm,
    coef_hbm,
    mixing_hbm,
    count_hbm,
    source_hbm,
    weight_hbm,
    target_hbm,
    mixed_hbm,
    flux_hbm,
    ext,
    blended,
    mixing,
    count,
    flux,
    nbr,
    coef,
    raw_source,
    raw_weight,
    raw_target,
    source,
    weight,
    target,
    table,
    sendbuf,
    recvbuf,
    split,
    mixed,
    total,
    in_sems,
    halo_send_sems,
    halo_recv_sems,
    send_sem,
    recv_sems,
    out_sems,
    flux_sem,
):
    comp, me = lax.axis_index("comp"), lax.axis_index("dom")
    other = 1 - comp
    right, left = lax.rem(me + 1, PEERS), lax.rem(me + PEERS - 1, PEERS)

    def load(i, src, dst):
        return pltpu.make_async_copy(src, dst, in_sems.at[i])

    inner = pl.ds(HALO, CELLS)
    state_loads = [
        load(h, state_hbm.at[0, :, pl.ds(8 * h, 8), :], ext.at[:, pl.ds(8 * h, 8), inner])
        for h in range(2)
    ]
    source_load = load(2, source_hbm.at[0, 0], raw_source)
    weight_load = load(3, weight_hbm.at[0, 0], raw_weight)
    count_load = load(4, count_hbm.at[0], count)
    early = [state_loads[0], source_load, weight_load, count_load]
    mixing_load = load(5, mixing_hbm.at[0], mixing)
    target_load = load(6, target_hbm.at[0, 0], raw_target)
    stencil_loads = [load(7, neighbours_hbm.at[0], nbr), load(8, coef_hbm.at[0], coef)]
    late = [state_loads[1], mixing_load, *stencil_loads, target_load]
    for one_load in early + late:
        one_load.start()

    barrier = pltpu.get_barrier_semaphore()

    def greet(step, c):
        pl.semaphore_signal(barrier, inc=1, device_id=(other, step), device_id_type=MESH)
        return c

    lax.fori_loop(0, PEERS, greet, 0)
    for side in (left, right):
        pl.semaphore_signal(barrier, inc=1, device_id=(comp, side), device_id_type=MESH)

    state_loads[0].wait()
    for v in range(VARS):
        for b in range(BLOCKS):
            table[v * BLOCKS + b : v * BLOCKS + b + 1, :] = ext[
                v, 0:1, HALO + b * LANES : HALO + (b + 1) * LANES
            ]
    table_halves = jnp.concatenate(halves(table[...]), axis=1)

    source_load.wait()
    weight_load.wait()
    count_load.wait()

    def by_peer(raw, tidy):
        for g in range(PEERS // 8):
            for c in range(CHUNKS):
                tidy[pl.ds(g * 8 * CHUNKS + c, 8, stride=CHUNKS), :] = raw[
                    g * 8 : g * 8 + 8, c * LANES : (c + 1) * LANES
                ]

    by_peer(raw_source, source)
    by_peer(raw_weight, weight)

    halos = [
        pltpu.make_async_remote_copy(
            src_ref=state_hbm.at[0, :, :, pl.ds(start, HALO)],
            dst_ref=ext.at[:, :, pl.ds(place, HALO)],
            send_sem=halo_send_sems.at[i],
            recv_sem=halo_recv_sems.at[i],
            device_id=(comp, side),
            device_id_type=MESH,
        )
        for i, (start, place, side) in enumerate(
            ((CELLS - HALO, FROM_LEFT, right), (0, FROM_RIGHT, left))
        )
    ]

    sublane = lax.broadcasted_iota(I32, (8, LANES), 0)
    lane = lax.broadcasted_iota(I32, (8, LANES), 1)
    slot = sublane * LANES + lane
    lane_rows = lax.broadcasted_iota(I32, (LANES, 1), 0).astype(I16)
    block_rows = lax.broadcasted_iota(I32, (BLOCKS, 1), 0).astype(I16)
    one, nought = BF16(1), BF16(0)

    ahead, behind = places(me, 1), places(me, -1)

    def to_peer(q, group):
        return pltpu.make_async_remote_copy(
            src_ref=sendbuf.at[q],
            dst_ref=recvbuf.at[me],
            send_sem=send_sem,
            recv_sem=recv_sems.at[group],
            device_id=(other, q),
            device_id_type=MESH,
        )

    def many(count, group):
        return pltpu.make_async_remote_copy(
            src_ref=sendbuf.at[pl.ds(0, count)],
            dst_ref=recvbuf.at[pl.ds(0, count)],
            send_sem=send_sem,
            recv_sem=recv_sems.at[group],
            device_id=(other, me),
            device_id_type=MESH,
        )

    def gather_one(q):
        cells = source[pl.ds(pl.multiple_of(q * CHUNKS, CHUNKS), CHUNKS), :]
        low, high = cells & (LANES - 1), cells >> 7
        used = jnp.where(
            slot < count[0, q],
            weight[pl.ds(pl.multiple_of(q * CHUNKS, CHUNKS), CHUNKS), :],
            0.0,
        )
        out = [jnp.zeros((8, LANES), F32) for _ in range(VARS)]
        for n in range(CHUNKS // 2):
            lows = jnp.concatenate([low[2 * n : 2 * n + 1], low[2 * n + 1 : 2 * n + 2]], axis=1)
            hot = jnp.where(lane_rows == lows.astype(I16), one, nought)
            rows = jnp.dot(
                table_halves,
                jnp.concatenate([hot, hot], axis=0),
                preferred_element_type=F32,
            )
            for half in range(2):
                c = 2 * n + half
                row = jnp.broadcast_to(high[c : c + 1], (8, LANES))
                within, group = row & 7, row >> 3
                for v in range(VARS):
                    picks = [
                        sublane_pick(
                            rows[
                                v * BLOCKS + t * 8 : v * BLOCKS + t * 8 + 8,
                                half * LANES : (half + 1) * LANES,
                            ],
                            within,
                        )
                        for t in range(BLOCKS // 8)
                    ]
                    pick = jnp.where(
                        group < 2,
                        jnp.where(group == 0, picks[0], picks[1]),
                        jnp.where(group == 2, picks[2], picks[3]),
                    )
                    out[v] = jnp.where(sublane == c, pick, out[v])
        for v in range(VARS):
            sendbuf[q, v * 8 : v * 8 + 8, :] = out[v] * used

    def gather(group, c_):
        peers = [peer_at(ahead, group, k) for k in range(BATCH)]
        for q in peers:
            gather_one(q)

        @pl.when(group == 0)
        def _():
            pl.semaphore_wait(barrier, PEERS + 2)
            for halo in halos:
                halo.start()

        for q in peers:
            to_peer(q, group).start()
        return c_

    lax.fori_loop(0, PEERS // BATCH, gather, 0)

    mixing_load.wait()
    spread = (
        lax.rem(lax.broadcasted_iota(I32, (ROWS, LEV), 0), LEV)
        == lax.broadcasted_iota(I32, (ROWS, LEV), 1)
    ).astype(F32)
    tiled = lax.dot_general(
        jnp.dot(spread, mixing[...], precision=lax.Precision.HIGHEST, preferred_element_type=F32),
        spread,
        (((1,), (1,)), ((), ())),
        precision=lax.Precision.HIGHEST,
        preferred_element_type=F32,
    )
    same = lax.div(lax.broadcasted_iota(I32, (ROWS, ROWS), 0), LEV) == lax.div(
        lax.broadcasted_iota(I32, (ROWS, ROWS), 1), LEV
    )
    mix_high, mix_low = halves(jnp.where(same, tiled, 0.0))
    mix_both = jnp.concatenate(
        [
            jnp.concatenate([mix_high, mix_high], axis=1),
            jnp.concatenate([mix_low, mix_low], axis=1),
        ],
        axis=0,
    )

    state_loads[1].wait()
    for halo in halos:
        halo.wait_recv()

    def blend(i, c_):
        cells = pl.ds(pl.multiple_of(i * 4 * LANES, 4 * LANES), 4 * LANES)
        both = jnp.concatenate(
            [halves(ext[v, :, cells])[part] for part in range(2) for v in range(VARS)], axis=0
        )
        result = jnp.dot(mix_both, both, preferred_element_type=F32)
        result = result[0:ROWS] + result[ROWS : 2 * ROWS]
        for v in range(VARS):
            blended[v, :, cells] = result[v * LEV : (v + 1) * LEV]
        high, low = halves(result)
        for e in range(4):
            at = pl.ds(pl.multiple_of((i * 4 + e) * ROWS, ROWS), ROWS)
            split[at, 0:LANES] = high[:, e * LANES : (e + 1) * LANES]
            split[at, LANES : 2 * LANES] = low[:, e * LANES : (e + 1) * LANES]
        return c_

    lax.fori_loop(0, (BLOCKS + SPAN - 1) // 4, blend, 0, unroll=3)
    for one_load in stencil_loads:
        one_load.wait()

    def rows_at(r, cells):
        return blended[r // 2, (r % 2) * 8 : (r % 2) * 8 + 8, cells]

    def stencil(b, c_):
        base = pl.multiple_of(b * LANES, LANES)
        window = split[pl.ds(pl.multiple_of(b * ROWS, ROWS), SPAN * ROWS), :]
        coefs = coef[:, pl.ds(base, LANES)]
        place = lane + nbr[:, pl.ds(base, LANES)]
        at, block = (place & (LANES - 1)), place >> 7
        rest = 1.0 - jnp.sum(coefs, axis=0, keepdims=True)
        acc = [rest * rows_at(r, pl.ds(HALO + base, LANES)) for r in range(ROWS // 8)]
        for pair in range(PRODUCTS // 2):
            hot = jnp.concatenate(
                [
                    jnp.where(lane_rows == at[j : j + 1].astype(I16), one, nought)
                    for j in (2 * pair, 2 * pair + 1)
                ],
                axis=1,
            )
            rows = jnp.dot(
                window, jnp.concatenate([hot, hot], axis=0), preferred_element_type=F32
            )
            for half in range(2):
                j = 2 * pair + half
                factor = jnp.broadcast_to(coefs[j : j + 1], (8, LANES))
                which = jnp.broadcast_to(block[j : j + 1], (8, LANES))
                lanes = slice(half * LANES, (half + 1) * LANES)
                for r in range(ROWS // 8):
                    pick = rows[r * 8 : r * 8 + 8, lanes]
                    for s in range(1, SPAN):
                        row = s * ROWS + r * 8
                        pick = jnp.where(which == s, rows[row : row + 8, lanes], pick)
                    acc[r] = acc[r] + factor * pick
        for r in range(ROWS // 8):
            mixed[r // 2, (r % 2) * 8 : (r % 2) * 8 + 8, pl.ds(base, LANES)] = acc[r]
        return c_

    lax.fori_loop(0, BLOCKS, stencil, 0, unroll=STENCIL_UNROLL)

    def permuted(b, rows):
        base = pl.multiple_of(b * LANES, LANES)
        cells = pl.ds(base, LANES)
        coefs = coef[:, cells]
        place = lane + nbr[:, cells]
        at, block = (place & (LANES - 1)), place >> 7
        acc = [mixed[r // 2, (r % 2) * 8 : (r % 2) * 8 + 8, cells] for r in rows]
        for j in range(PRODUCTS, NBR):
            turn = jnp.broadcast_to(at[j : j + 1], (8, LANES))
            which = jnp.broadcast_to(block[j : j + 1], (8, LANES))
            factor = jnp.broadcast_to(coefs[j : j + 1], (8, LANES))
            for i, r in enumerate(rows):
                pick = lane_pick(rows_at(r, cells), turn)
                for s in range(1, SPAN):
                    other_pick = lane_pick(rows_at(r, pl.ds(base + s * LANES, LANES)), turn)
                    pick = jnp.where(which == s, other_pick, pick)
                acc[i] = acc[i] + factor * pick
        for i, r in enumerate(rows):
            mixed[r // 2, (r % 2) * 8 : (r % 2) * 8 + 8, cells] = acc[i]

    target_load.wait()
    by_peer(raw_target, target)
    total[...] = jnp.zeros_like(total)

    def scatter_one(p):
        cells = target[pl.ds(pl.multiple_of(p * CHUNKS, CHUNKS), CHUNKS), :]
        low, high = (cells & (LANES - 1)), (cells >> 7)
        values, hots = [], []
        for c in range(CHUNKS):
            here = block_rows == high[c : c + 1].astype(I16)
            hots.append(jnp.where(lane_rows == low[c : c + 1].astype(I16), one, nought))
            parts = [halves(recvbuf[p, v * 8 + c : v * 8 + c + 1, :]) for v in range(VARS)]
            values.append(
                jnp.concatenate(
                    [jnp.where(here, parts[v][i], nought) for i in range(2) for v in range(VARS)],
                    axis=0,
                )
            )
        total[...] += lax.dot_general(
            jnp.concatenate(values, axis=1),
            jnp.concatenate(hots, axis=1),
            (((1,), (1,)), ((), ())),
            preferred_element_type=F32,
        )

    def store_of(group):
        width = CELLS * BATCH // PEERS
        cells = pl.ds(pl.multiple_of(group * width, width), width)
        return pltpu.make_async_copy(
            mixed.at[:, :, cells], mixed_hbm.at[:, :, cells], out_sems.at[group]
        )

    def scatter(group, c_):
        peers = [peer_at(behind, group, k) for k in range(BATCH)]
        many(BATCH, group).wait_recv()
        for k, p in enumerate(peers):
            scatter_one(p)
            half = ROWS // 16
            permuted(group * (BATCH // 2) + k // 2, range(k % 2 * half, (k % 2 + 1) * half))
        store_of(group).start()
        return c_

    lax.fori_loop(0, PEERS // BATCH, scatter, 0)

    for v in range(VARS):
        for b in range(BLOCKS):
            r = v * BLOCKS + b
            flux[v : v + 1, b * LANES : (b + 1) * LANES] = (
                total[r : r + 1, :] + total[r + VARS * BLOCKS : r + VARS * BLOCKS + 1, :]
            )

    flux_store = pltpu.make_async_copy(flux, flux_hbm, flux_sem)
    flux_store.start()

    many(PEERS, 0).wait_send()
    for halo in halos:
        halo.wait_send()
    for group in range(PEERS // BATCH):
        store_of(group).wait()
    flux_store.wait()


def finish(
    mixed_hbm, flux_in, mixing_hbm, updated_hbm, flux_out, state, flux, mixing, load_sems, store_sems
):
    loads = [
        pltpu.make_async_copy(mixed_hbm.at[v], state.at[v], load_sems.at[v]) for v in range(VARS)
    ]
    flux_load = pltpu.make_async_copy(flux_in, flux, load_sems.at[VARS])
    mixing_load = pltpu.make_async_copy(mixing_hbm.at[0], mixing, load_sems.at[VARS + 1])
    for load in [flux_load, mixing_load, *loads]:
        load.start()
    flux_load.wait()
    mixing_load.wait()
    flux_store = pltpu.make_async_copy(flux, flux_out.at[0], store_sems.at[VARS])
    flux_store.start()
    stores = []
    shares = [
        jnp.broadcast_to(mixing[h * 8 : h * 8 + 8, 0:1], (8, LANES)) for h in range(LEV // 8)
    ]
    for v in range(VARS):
        loads[v].wait()
        for b in range(BLOCKS):
            cells = slice(b * LANES, (b + 1) * LANES)
            row = jnp.broadcast_to(flux[v : v + 1, cells], (8, LANES))
            for h in range(LEV // 8):
                levels = slice(h * 8, h * 8 + 8)
                state[v, levels, cells] = state[v, levels, cells] + shares[h] * row
        store = pltpu.make_async_copy(state.at[v], updated_hbm.at[0, v], store_sems.at[v])
        store.start()
        stores.append(store)
    for store in stores:
        store.wait()
    flux_store.wait()


def local(
    model_state,
    neighbours,
    stencil_coef,
    column_mixing_operator,
    remap_count,
    remap_source,
    remap_weight,
    remap_target,
):
    hbm = pl.BlockSpec(memory_space=pltpu.HBM)
    mixed, flux = pl.pallas_call(
        kernel,
        out_shape=(
            jax.ShapeDtypeStruct((VARS, LEV, CELLS), F32),
            jax.ShapeDtypeStruct((VARS, CELLS), F32),
        ),
        in_specs=[hbm] * 8,
        out_specs=(hbm, hbm),
        scratch_shapes=[
            pltpu.VMEM((VARS, LEV, CELLS + 2 * HALO), F32),
            pltpu.VMEM((VARS, LEV, CELLS + 2 * HALO), F32),
            pltpu.VMEM((LEV, LEV), F32),
            pltpu.SMEM((1, PEERS), I32),
            pltpu.VMEM((VARS, CELLS), F32),
            pltpu.VMEM((NBR, CELLS), I32),
            pltpu.VMEM((NBR, CELLS), F32),
            pltpu.VMEM((PEERS, CAP), I32),
            pltpu.VMEM((PEERS, CAP), F32),
            pltpu.VMEM((PEERS, CAP), I32),
            pltpu.VMEM((PEERS * CHUNKS, LANES), I32),
            pltpu.VMEM((PEERS * CHUNKS, LANES), F32),
            pltpu.VMEM((PEERS * CHUNKS, LANES), I32),
            pltpu.VMEM((VARS * BLOCKS, LANES), F32),
            pltpu.VMEM((PEERS, VARS * CHUNKS, LANES), F32),
            pltpu.VMEM((PEERS, VARS * CHUNKS, LANES), F32),
            pltpu.VMEM(((BLOCKS + SPAN - 1) * ROWS, 2 * LANES), BF16),
            pltpu.VMEM((VARS, LEV, CELLS), F32),
            pltpu.VMEM((2 * VARS * BLOCKS, LANES), F32),
            pltpu.SemaphoreType.DMA((9,)),
            pltpu.SemaphoreType.DMA((2,)),
            pltpu.SemaphoreType.DMA((2,)),
            pltpu.SemaphoreType.DMA,
            pltpu.SemaphoreType.DMA((PEERS // BATCH,)),
            pltpu.SemaphoreType.DMA((PEERS // BATCH,)),
            pltpu.SemaphoreType.DMA,
        ],
        compiler_params=pltpu.CompilerParams(
            collective_id=0, has_side_effects=True, vmem_limit_bytes=60 << 20
        ),
        name="step",
    )(
        model_state,
        neighbours,
        stencil_coef,
        column_mixing_operator,
        remap_count,
        remap_source,
        remap_weight,
        remap_target,
    )
    return pl.pallas_call(
        finish,
        out_shape=(
            jax.ShapeDtypeStruct((1, VARS, LEV, CELLS), F32),
            jax.ShapeDtypeStruct((1, VARS, CELLS), F32),
        ),
        in_specs=[hbm] * 3,
        out_specs=(hbm, hbm),
        scratch_shapes=[
            pltpu.VMEM((VARS, LEV, CELLS), F32),
            pltpu.VMEM((VARS, CELLS), F32),
            pltpu.VMEM((LEV, LEV), F32),
            pltpu.SemaphoreType.DMA((VARS + 2,)),
            pltpu.SemaphoreType.DMA((VARS + 1,)),
        ],
        compiler_params=pltpu.CompilerParams(vmem_limit_bytes=60 << 20),
        name="finish",
    )(mixed, flux, column_mixing_operator)


def solution(mesh):
    in_specs = (
        P("comp", None, None, "dom"),
        P("comp", None, "dom"),
        P("comp", None, "dom"),
        P("comp", None, None),
        P("comp", "dom", None),
        P("comp", "dom", None, None),
        P("comp", "dom", None, None),
        P("comp", "dom", None, None),
    )
    out_specs = (P("comp", None, None, "dom"), P("comp", None, "dom"))
    return jax.shard_map(local, mesh=mesh, in_specs=in_specs, out_specs=out_specs, check_vma=False)
```

```python
import itertools
import random

import jax
import jax.numpy as jnp
from jax import lax
from jax.experimental import pallas as pl
from jax.experimental.pallas import tpu as pltpu
from jax.sharding import PartitionSpec as P

MESH = pl.DeviceIdType.MESH
F32, BF16, I32, I16 = jnp.float32, jnp.bfloat16, jnp.int32, jnp.int16
LANES = 128
SIDE = 4
PEERS = SIDE**3
VARS, LEV, NBR = 4, 16, 8
CELLS = 4096
CAP = 1024
HALO = 256
BLOCKS = CELLS // LANES
CHUNKS = CAP // LANES
ROWS = VARS * LEV
SPAN = 2 * HALO // LANES + 1
BATCH = 16
SENT = 8
STENCIL_UNROLL = 4
PRODUCTS = 4
FROM_LEFT, FROM_RIGHT = 0, HALO + CELLS


def halves(x):
    high = x.astype(BF16)
    return high, (x - high.astype(F32)).astype(BF16)


def lane_pick(table, index):
    return jnp.take_along_axis(table, index, axis=1, mode="promise_in_bounds")


def sublane_pick(table, index):
    return jnp.take_along_axis(table, index, axis=0, mode="promise_in_bounds")


def displacements():
    moves = list(itertools.product((0, 1, 2, -1), repeat=3))
    random.Random(1).shuffle(moves)
    ordered = []
    for move in moves:
        for one in (move, tuple(-m if m != 2 else 2 for m in move)):
            if one not in ordered:
                ordered.append(one)
    ordered.sort(key=lambda move: sum(abs(m) for m in move))
    return [tuple(m % SIDE for m in move) for move in ordered]


ORDER = displacements()


def places(me, sign):
    return [
        [
            unit * lax.rem(lax.rem(lax.div(me, unit), SIDE) + sign * move + SIDE, SIDE)
            for move in range(SIDE)
        ]
        for unit in (SIDE * SIDE, SIDE, 1)
    ]


def peer_at(places_, group, batch, k):
    place = 0
    for g in range(PEERS // batch):
        there = sum(places_[axis][move] for axis, move in enumerate(ORDER[g * batch + k]))
        place = there if g == 0 else jnp.where(group == g, there, place)
    return place


def kernel(
    state_hbm,
    neighbours_hbm,
    coef_hbm,
    mixing_hbm,
    count_hbm,
    source_hbm,
    weight_hbm,
    target_hbm,
    mixed_hbm,
    flux_hbm,
    ext,
    blended,
    mixing,
    count,
    flux,
    nbr,
    coef,
    raw_source,
    raw_weight,
    raw_target,
    source,
    weight,
    target,
    table,
    sendbuf,
    recvbuf,
    split,
    mixed,
    total,
    in_sems,
    halo_send_sems,
    halo_recv_sems,
    send_sem,
    recv_sems,
    out_sems,
    flux_sem,
):
    comp, me = lax.axis_index("comp"), lax.axis_index("dom")
    other = 1 - comp
    right, left = lax.rem(me + 1, PEERS), lax.rem(me + PEERS - 1, PEERS)

    def load(i, src, dst):
        return pltpu.make_async_copy(src, dst, in_sems.at[i])

    inner = pl.ds(HALO, CELLS)
    state_loads = [
        load(h, state_hbm.at[0, :, pl.ds(8 * h, 8), :], ext.at[:, pl.ds(8 * h, 8), inner])
        for h in range(2)
    ]
    source_load = load(2, source_hbm.at[0, 0], raw_source)
    weight_load = load(3, weight_hbm.at[0, 0], raw_weight)
    count_load = load(4, count_hbm.at[0], count)
    early = [state_loads[0], source_load, weight_load, count_load]
    mixing_load = load(5, mixing_hbm.at[0], mixing)
    target_load = load(6, target_hbm.at[0, 0], raw_target)
    stencil_loads = [load(7, neighbours_hbm.at[0], nbr), load(8, coef_hbm.at[0], coef)]
    late = [state_loads[1], mixing_load, *stencil_loads, target_load]
    for one_load in early + late:
        one_load.start()

    barrier = pltpu.get_barrier_semaphore()

    def greet(step, c):
        pl.semaphore_signal(barrier, inc=1, device_id=(other, step), device_id_type=MESH)
        return c

    lax.fori_loop(0, PEERS, greet, 0)
    for side in (left, right):
        pl.semaphore_signal(barrier, inc=1, device_id=(comp, side), device_id_type=MESH)

    state_loads[0].wait()
    for v in range(VARS):
        for b in range(BLOCKS):
            table[v * BLOCKS + b : v * BLOCKS + b + 1, :] = ext[
                v, 0:1, HALO + b * LANES : HALO + (b + 1) * LANES
            ]
    table_halves = jnp.concatenate(halves(table[...]), axis=1)

    source_load.wait()
    weight_load.wait()
    count_load.wait()

    def by_peer(raw, tidy):
        for g in range(PEERS // 8):
            for c in range(CHUNKS):
                tidy[pl.ds(g * 8 * CHUNKS + c, 8, stride=CHUNKS), :] = raw[
                    g * 8 : g * 8 + 8, c * LANES : (c + 1) * LANES
                ]

    by_peer(raw_source, source)
    by_peer(raw_weight, weight)

    halos = [
        pltpu.make_async_remote_copy(
            src_ref=state_hbm.at[0, :, :, pl.ds(start, HALO)],
            dst_ref=ext.at[:, :, pl.ds(place, HALO)],
            send_sem=halo_send_sems.at[i],
            recv_sem=halo_recv_sems.at[i],
            device_id=(comp, side),
            device_id_type=MESH,
        )
        for i, (start, place, side) in enumerate(
            ((CELLS - HALO, FROM_LEFT, right), (0, FROM_RIGHT, left))
        )
    ]

    sublane = lax.broadcasted_iota(I32, (8, LANES), 0)
    lane = lax.broadcasted_iota(I32, (8, LANES), 1)
    slot = sublane * LANES + lane
    lane_rows = lax.broadcasted_iota(I32, (LANES, 1), 0).astype(I16)
    block_rows = lax.broadcasted_iota(I32, (BLOCKS, 1), 0).astype(I16)
    one, nought = BF16(1), BF16(0)

    ahead, behind = places(me, 1), places(me, -1)

    def to_peer(q, group):
        return pltpu.make_async_remote_copy(
            src_ref=sendbuf.at[q],
            dst_ref=recvbuf.at[me],
            send_sem=send_sem,
            recv_sem=recv_sems.at[group],
            device_id=(other, q),
            device_id_type=MESH,
        )

    def many(count, group):
        return pltpu.make_async_remote_copy(
            src_ref=sendbuf.at[pl.ds(0, count)],
            dst_ref=recvbuf.at[pl.ds(0, count)],
            send_sem=send_sem,
            recv_sem=recv_sems.at[group],
            device_id=(other, me),
            device_id_type=MESH,
        )

    def gather_one(q):
        cells = source[pl.ds(pl.multiple_of(q * CHUNKS, CHUNKS), CHUNKS), :]
        low, high = cells & (LANES - 1), cells >> 7
        used = jnp.where(
            slot < count[0, q],
            weight[pl.ds(pl.multiple_of(q * CHUNKS, CHUNKS), CHUNKS), :],
            0.0,
        )
        out = [jnp.zeros((8, LANES), F32) for _ in range(VARS)]
        for n in range(CHUNKS // 2):
            lows = jnp.concatenate([low[2 * n : 2 * n + 1], low[2 * n + 1 : 2 * n + 2]], axis=1)
            hot = jnp.where(lane_rows == lows.astype(I16), one, nought)
            rows = jnp.dot(
                table_halves,
                jnp.concatenate([hot, hot], axis=0),
                preferred_element_type=F32,
            )
            for half in range(2):
                c = 2 * n + half
                row = jnp.broadcast_to(high[c : c + 1], (8, LANES))
                within, group = row & 7, row >> 3
                for v in range(VARS):
                    picks = [
                        sublane_pick(
                            rows[
                                v * BLOCKS + t * 8 : v * BLOCKS + t * 8 + 8,
                                half * LANES : (half + 1) * LANES,
                            ],
                            within,
                        )
                        for t in range(BLOCKS // 8)
                    ]
                    pick = jnp.where(
                        group < 2,
                        jnp.where(group == 0, picks[0], picks[1]),
                        jnp.where(group == 2, picks[2], picks[3]),
                    )
                    out[v] = jnp.where(sublane == c, pick, out[v])
        for v in range(VARS):
            sendbuf[q, v * 8 : v * 8 + 8, :] = out[v] * used

    def gather(group, c_):
        peers = [peer_at(ahead, group, SENT, k) for k in range(SENT)]
        for q in peers:
            gather_one(q)

        @pl.when(group == 0)
        def _():
            pl.semaphore_wait(barrier, PEERS + 2)
            for halo in halos:
                halo.start()

        for q in peers:
            to_peer(q, lax.div(group, BATCH // SENT) + jnp.where(group == PEERS // SENT - 1, 1, 0)).start()
        return c_

    lax.fori_loop(0, PEERS // SENT, gather, 0)

    mixing_load.wait()
    spread = (
        lax.rem(lax.broadcasted_iota(I32, (ROWS, LEV), 0), LEV)
        == lax.broadcasted_iota(I32, (ROWS, LEV), 1)
    ).astype(F32)
    tiled = lax.dot_general(
        jnp.dot(spread, mixing[...], precision=lax.Precision.HIGHEST, preferred_element_type=F32),
        spread,
        (((1,), (1,)), ((), ())),
        precision=lax.Precision.HIGHEST,
        preferred_element_type=F32,
    )
    same = lax.div(lax.broadcasted_iota(I32, (ROWS, ROWS), 0), LEV) == lax.div(
        lax.broadcasted_iota(I32, (ROWS, ROWS), 1), LEV
    )
    mix_high, mix_low = halves(jnp.where(same, tiled, 0.0))
    mix_both = jnp.concatenate(
        [
            jnp.concatenate([mix_high, mix_high], axis=1),
            jnp.concatenate([mix_low, mix_low], axis=1),
        ],
        axis=0,
    )

    state_loads[1].wait()
    for halo in halos:
        halo.wait_recv()

    def blend(i, c_):
        cells = pl.ds(pl.multiple_of(i * 4 * LANES, 4 * LANES), 4 * LANES)
        both = jnp.concatenate(
            [halves(ext[v, :, cells])[part] for part in range(2) for v in range(VARS)], axis=0
        )
        result = jnp.dot(mix_both, both, preferred_element_type=F32)
        result = result[0:ROWS] + result[ROWS : 2 * ROWS]
        for v in range(VARS):
            blended[v, :, cells] = result[v * LEV : (v + 1) * LEV]
        high, low = halves(result)
        for e in range(4):
            at = pl.ds(pl.multiple_of((i * 4 + e) * ROWS, ROWS), ROWS)
            split[at, 0:LANES] = high[:, e * LANES : (e + 1) * LANES]
            split[at, LANES : 2 * LANES] = low[:, e * LANES : (e + 1) * LANES]
        return c_

    lax.fori_loop(0, (BLOCKS + SPAN - 1) // 4, blend, 0, unroll=3)
    for one_load in stencil_loads:
        one_load.wait()

    def rows_at(r, cells):
        return blended[r // 2, (r % 2) * 8 : (r % 2) * 8 + 8, cells]

    def stencil(b, c_):
        base = pl.multiple_of(b * LANES, LANES)
        window = split[pl.ds(pl.multiple_of(b * ROWS, ROWS), SPAN * ROWS), :]
        coefs = coef[:, pl.ds(base, LANES)]
        place = lane + nbr[:, pl.ds(base, LANES)]
        at, block = (place & (LANES - 1)), place >> 7
        rest = 1.0 - jnp.sum(coefs, axis=0, keepdims=True)
        acc = [rest * rows_at(r, pl.ds(HALO + base, LANES)) for r in range(ROWS // 8)]
        for pair in range(PRODUCTS // 2):
            hot = jnp.concatenate(
                [
                    jnp.where(lane_rows == at[j : j + 1].astype(I16), one, nought)
                    for j in (2 * pair, 2 * pair + 1)
                ],
                axis=1,
            )
            rows = jnp.dot(
                window, jnp.concatenate([hot, hot], axis=0), preferred_element_type=F32
            )
            for half in range(2):
                j = 2 * pair + half
                factor = jnp.broadcast_to(coefs[j : j + 1], (8, LANES))
                which = jnp.broadcast_to(block[j : j + 1], (8, LANES))
                lanes = slice(half * LANES, (half + 1) * LANES)
                for r in range(ROWS // 8):
                    pick = rows[r * 8 : r * 8 + 8, lanes]
                    for s in range(1, SPAN):
                        row = s * ROWS + r * 8
                        pick = jnp.where(which == s, rows[row : row + 8, lanes], pick)
                    acc[r] = acc[r] + factor * pick
        for r in range(ROWS // 8):
            mixed[r // 2, (r % 2) * 8 : (r % 2) * 8 + 8, pl.ds(base, LANES)] = acc[r]
        return c_

    lax.fori_loop(0, BLOCKS, stencil, 0, unroll=STENCIL_UNROLL)

    def permuted(b, rows):
        base = pl.multiple_of(b * LANES, LANES)
        cells = pl.ds(base, LANES)
        coefs = coef[:, cells]
        place = lane + nbr[:, cells]
        at, block = (place & (LANES - 1)), place >> 7
        acc = [mixed[r // 2, (r % 2) * 8 : (r % 2) * 8 + 8, cells] for r in rows]
        for j in range(PRODUCTS, NBR):
            turn = jnp.broadcast_to(at[j : j + 1], (8, LANES))
            which = jnp.broadcast_to(block[j : j + 1], (8, LANES))
            factor = jnp.broadcast_to(coefs[j : j + 1], (8, LANES))
            for i, r in enumerate(rows):
                pick = lane_pick(rows_at(r, cells), turn)
                for s in range(1, SPAN):
                    other_pick = lane_pick(rows_at(r, pl.ds(base + s * LANES, LANES)), turn)
                    pick = jnp.where(which == s, other_pick, pick)
                acc[i] = acc[i] + factor * pick
        for i, r in enumerate(rows):
            mixed[r // 2, (r % 2) * 8 : (r % 2) * 8 + 8, cells] = acc[i]

    target_load.wait()
    by_peer(raw_target, target)
    total[...] = jnp.zeros_like(total)

    def scatter_one(p):
        cells = target[pl.ds(pl.multiple_of(p * CHUNKS, CHUNKS), CHUNKS), :]
        low, high = (cells & (LANES - 1)), (cells >> 7)
        values, hots = [], []
        for c in range(CHUNKS):
            here = block_rows == high[c : c + 1].astype(I16)
            hots.append(jnp.where(lane_rows == low[c : c + 1].astype(I16), one, nought))
            parts = [halves(recvbuf[p, v * 8 + c : v * 8 + c + 1, :]) for v in range(VARS)]
            values.append(
                jnp.concatenate(
                    [jnp.where(here, parts[v][i], nought) for i in range(2) for v in range(VARS)],
                    axis=0,
                )
            )
        total[...] += lax.dot_general(
            jnp.concatenate(values, axis=1),
            jnp.concatenate(hots, axis=1),
            (((1,), (1,)), ((), ())),
            preferred_element_type=F32,
        )

    def store_of(group):
        width = CELLS * BATCH // PEERS
        cells = pl.ds(pl.multiple_of(group * width, width), width)
        return pltpu.make_async_copy(
            mixed.at[:, :, cells], mixed_hbm.at[:, :, cells], out_sems.at[group]
        )

    def arrived(group, batch, sem):
        peers = [peer_at(behind, group, batch, k) for k in range(batch)]
        many(batch, sem).wait_recv()
        half = ROWS // 16
        for k, p in enumerate(peers):
            scatter_one(p)
            permuted(group * (batch // 2) + k // 2, range(k % 2 * half, (k % 2 + 1) * half))

    last = PEERS // BATCH - 1

    def scatter(group, c_):
        arrived(group, BATCH, group)
        store_of(group).start()
        return c_

    lax.fori_loop(0, last, scatter, 0)

    def scatter_last(part, c_):
        arrived(part + last * (BATCH // SENT), SENT, part + last)
        return c_

    lax.fori_loop(0, BATCH // SENT, scatter_last, 0)
    store_of(last).start()

    for v in range(VARS):
        for b in range(BLOCKS):
            r = v * BLOCKS + b
            flux[v : v + 1, b * LANES : (b + 1) * LANES] = (
                total[r : r + 1, :] + total[r + VARS * BLOCKS : r + VARS * BLOCKS + 1, :]
            )

    flux_store = pltpu.make_async_copy(flux, flux_hbm, flux_sem)
    flux_store.start()

    many(PEERS, 0).wait_send()
    for halo in halos:
        halo.wait_send()
    for group in range(PEERS // BATCH):
        store_of(group).wait()
    flux_store.wait()


def finish(
    mixed_hbm, flux_in, mixing_hbm, updated_hbm, flux_out, state, flux, mixing, load_sems, store_sems
):
    loads = [
        pltpu.make_async_copy(mixed_hbm.at[v], state.at[v], load_sems.at[v]) for v in range(VARS)
    ]
    flux_load = pltpu.make_async_copy(flux_in, flux, load_sems.at[VARS])
    mixing_load = pltpu.make_async_copy(mixing_hbm.at[0], mixing, load_sems.at[VARS + 1])
    for load in [flux_load, mixing_load, *loads]:
        load.start()
    flux_load.wait()
    mixing_load.wait()
    flux_store = pltpu.make_async_copy(flux, flux_out.at[0], store_sems.at[VARS])
    flux_store.start()
    stores = []
    shares = [
        jnp.broadcast_to(mixing[h * 8 : h * 8 + 8, 0:1], (8, LANES)) for h in range(LEV // 8)
    ]
    for v in range(VARS):
        loads[v].wait()
        for b in range(BLOCKS):
            cells = slice(b * LANES, (b + 1) * LANES)
            row = jnp.broadcast_to(flux[v : v + 1, cells], (8, LANES))
            for h in range(LEV // 8):
                levels = slice(h * 8, h * 8 + 8)
                state[v, levels, cells] = state[v, levels, cells] + shares[h] * row
        store = pltpu.make_async_copy(state.at[v], updated_hbm.at[0, v], store_sems.at[v])
        store.start()
        stores.append(store)
    for store in stores:
        store.wait()
    flux_store.wait()


def local(
    model_state,
    neighbours,
    stencil_coef,
    column_mixing_operator,
    remap_count,
    remap_source,
    remap_weight,
    remap_target,
):
    hbm = pl.BlockSpec(memory_space=pltpu.HBM)
    mixed, flux = pl.pallas_call(
        kernel,
        out_shape=(
            jax.ShapeDtypeStruct((VARS, LEV, CELLS), F32),
            jax.ShapeDtypeStruct((VARS, CELLS), F32),
        ),
        in_specs=[hbm] * 8,
        out_specs=(hbm, hbm),
        scratch_shapes=[
            pltpu.VMEM((VARS, LEV, CELLS + 2 * HALO), F32),
            pltpu.VMEM((VARS, LEV, CELLS + 2 * HALO), F32),
            pltpu.VMEM((LEV, LEV), F32),
            pltpu.SMEM((1, PEERS), I32),
            pltpu.VMEM((VARS, CELLS), F32),
            pltpu.VMEM((NBR, CELLS), I32),
            pltpu.VMEM((NBR, CELLS), F32),
            pltpu.VMEM((PEERS, CAP), I32),
            pltpu.VMEM((PEERS, CAP), F32),
            pltpu.VMEM((PEERS, CAP), I32),
            pltpu.VMEM((PEERS * CHUNKS, LANES), I32),
            pltpu.VMEM((PEERS * CHUNKS, LANES), F32),
            pltpu.VMEM((PEERS * CHUNKS, LANES), I32),
            pltpu.VMEM((VARS * BLOCKS, LANES), F32),
            pltpu.VMEM((PEERS, VARS * CHUNKS, LANES), F32),
            pltpu.VMEM((PEERS, VARS * CHUNKS, LANES), F32),
            pltpu.VMEM(((BLOCKS + SPAN - 1) * ROWS, 2 * LANES), BF16),
            pltpu.VMEM((VARS, LEV, CELLS), F32),
            pltpu.VMEM((2 * VARS * BLOCKS, LANES), F32),
            pltpu.SemaphoreType.DMA((9,)),
            pltpu.SemaphoreType.DMA((2,)),
            pltpu.SemaphoreType.DMA((2,)),
            pltpu.SemaphoreType.DMA,
            pltpu.SemaphoreType.DMA((PEERS // BATCH + 1,)),
            pltpu.SemaphoreType.DMA((PEERS // BATCH,)),
            pltpu.SemaphoreType.DMA,
        ],
        compiler_params=pltpu.CompilerParams(
            collective_id=0, has_side_effects=True, vmem_limit_bytes=60 << 20
        ),
        name="step",
    )(
        model_state,
        neighbours,
        stencil_coef,
        column_mixing_operator,
        remap_count,
        remap_source,
        remap_weight,
        remap_target,
    )
    return pl.pallas_call(
        finish,
        out_shape=(
            jax.ShapeDtypeStruct((1, VARS, LEV, CELLS), F32),
            jax.ShapeDtypeStruct((1, VARS, CELLS), F32),
        ),
        in_specs=[hbm] * 3,
        out_specs=(hbm, hbm),
        scratch_shapes=[
            pltpu.VMEM((VARS, LEV, CELLS), F32),
            pltpu.VMEM((VARS, CELLS), F32),
            pltpu.VMEM((LEV, LEV), F32),
            pltpu.SemaphoreType.DMA((VARS + 2,)),
            pltpu.SemaphoreType.DMA((VARS + 1,)),
        ],
        compiler_params=pltpu.CompilerParams(vmem_limit_bytes=60 << 20),
        name="finish",
    )(mixed, flux, column_mixing_operator)


def solution(mesh):
    in_specs = (
        P("comp", None, None, "dom"),
        P("comp", None, "dom"),
        P("comp", None, "dom"),
        P("comp", None, None),
        P("comp", "dom", None),
        P("comp", "dom", None, None),
        P("comp", "dom", None, None),
        P("comp", "dom", None, None),
    )
    out_specs = (P("comp", None, None, "dom"), P("comp", None, "dom"))
    return jax.shard_map(local, mesh=mesh, in_specs=in_specs, out_specs=out_specs, check_vma=False)
```

```python
import itertools
import random

import jax
import jax.numpy as jnp
from jax import lax
from jax.experimental import pallas as pl
from jax.experimental.pallas import tpu as pltpu
from jax.sharding import PartitionSpec as P

MESH = pl.DeviceIdType.MESH
F32, BF16, I32, I16 = jnp.float32, jnp.bfloat16, jnp.int32, jnp.int16
LANES = 128
SIDE = 4
PEERS = SIDE**3
VARS, LEV, NBR = 4, 16, 8
CELLS = 4096
CAP = 1024
HALO = 256
BLOCKS = CELLS // LANES
CHUNKS = CAP // LANES
ROWS = VARS * LEV
SPAN = 2 * HALO // LANES + 1
BATCH = 16
SENT = 8
STENCIL_UNROLL = 8
PRODUCTS = 4
FROM_LEFT, FROM_RIGHT = 0, HALO + CELLS


def halves(x):
    high = x.astype(BF16)
    return high, (x - high.astype(F32)).astype(BF16)


def lane_pick(table, index):
    return jnp.take_along_axis(table, index, axis=1, mode="promise_in_bounds")


def sublane_pick(table, index):
    return jnp.take_along_axis(table, index, axis=0, mode="promise_in_bounds")


def displacements():
    moves = list(itertools.product((0, 1, 2, -1), repeat=3))
    random.Random(1).shuffle(moves)
    ordered = []
    for move in moves:
        for one in (move, tuple(-m if m != 2 else 2 for m in move)):
            if one not in ordered:
                ordered.append(one)
    ordered.sort(key=lambda move: sum(abs(m) for m in move))
    return [tuple(m % SIDE for m in move) for move in ordered]


ORDER = displacements()


def places(me, sign):
    return [
        [
            unit * lax.rem(lax.rem(lax.div(me, unit), SIDE) + sign * move + SIDE, SIDE)
            for move in range(SIDE)
        ]
        for unit in (SIDE * SIDE, SIDE, 1)
    ]


def peer_at(places_, group, batch, k):
    place = 0
    for g in range(PEERS // batch):
        there = sum(places_[axis][move] for axis, move in enumerate(ORDER[g * batch + k]))
        place = there if g == 0 else jnp.where(group == g, there, place)
    return place


def kernel(
    state_hbm,
    neighbours_hbm,
    coef_hbm,
    mixing_hbm,
    count_hbm,
    source_hbm,
    weight_hbm,
    target_hbm,
    mixed_hbm,
    flux_hbm,
    ext,
    blended,
    mixing,
    count,
    flux,
    nbr,
    coef,
    raw_source,
    raw_weight,
    raw_target,
    source,
    weight,
    target,
    table,
    sendbuf,
    recvbuf,
    split,
    mixed,
    total,
    in_sems,
    halo_send_sems,
    halo_recv_sems,
    send_sem,
    recv_sems,
    out_sems,
    flux_sem,
):
    comp, me = lax.axis_index("comp"), lax.axis_index("dom")
    other = 1 - comp
    right, left = lax.rem(me + 1, PEERS), lax.rem(me + PEERS - 1, PEERS)

    def load(i, src, dst):
        return pltpu.make_async_copy(src, dst, in_sems.at[i])

    inner = pl.ds(HALO, CELLS)
    state_loads = [
        load(h, state_hbm.at[0, :, pl.ds(8 * h, 8), :], ext.at[:, pl.ds(8 * h, 8), inner])
        for h in range(2)
    ]
    source_load = load(2, source_hbm.at[0, 0], raw_source)
    weight_load = load(3, weight_hbm.at[0, 0], raw_weight)
    count_load = load(4, count_hbm.at[0], count)
    early = [state_loads[0], source_load, weight_load, count_load]
    mixing_load = load(5, mixing_hbm.at[0], mixing)
    target_load = load(6, target_hbm.at[0, 0], raw_target)
    stencil_loads = [load(7, neighbours_hbm.at[0], nbr), load(8, coef_hbm.at[0], coef)]
    late = [state_loads[1], mixing_load, *stencil_loads, target_load]
    for one_load in early + late:
        one_load.start()

    barrier = pltpu.get_barrier_semaphore()

    def greet(step, c):
        pl.semaphore_signal(barrier, inc=1, device_id=(other, step), device_id_type=MESH)
        return c

    lax.fori_loop(0, PEERS, greet, 0)
    for side in (left, right):
        pl.semaphore_signal(barrier, inc=1, device_id=(comp, side), device_id_type=MESH)

    state_loads[0].wait()
    for v in range(VARS):
        for b in range(BLOCKS):
            table[v * BLOCKS + b : v * BLOCKS + b + 1, :] = ext[
                v, 0:1, HALO + b * LANES : HALO + (b + 1) * LANES
            ]
    table_halves = jnp.concatenate(halves(table[...]), axis=1)

    source_load.wait()
    weight_load.wait()
    count_load.wait()

    def by_peer(raw, tidy):
        for g in range(PEERS // 8):
            for c in range(CHUNKS):
                tidy[pl.ds(g * 8 * CHUNKS + c, 8, stride=CHUNKS), :] = raw[
                    g * 8 : g * 8 + 8, c * LANES : (c + 1) * LANES
                ]

    by_peer(raw_source, source)
    by_peer(raw_weight, weight)

    halos = [
        pltpu.make_async_remote_copy(
            src_ref=state_hbm.at[0, :, :, pl.ds(start, HALO)],
            dst_ref=ext.at[:, :, pl.ds(place, HALO)],
            send_sem=halo_send_sems.at[i],
            recv_sem=halo_recv_sems.at[i],
            device_id=(comp, side),
            device_id_type=MESH,
        )
        for i, (start, place, side) in enumerate(
            ((CELLS - HALO, FROM_LEFT, right), (0, FROM_RIGHT, left))
        )
    ]

    sublane = lax.broadcasted_iota(I32, (8, LANES), 0)
    lane = lax.broadcasted_iota(I32, (8, LANES), 1)
    slot = sublane * LANES + lane
    lane_rows = lax.broadcasted_iota(I32, (LANES, 1), 0).astype(I16)
    block_rows = lax.broadcasted_iota(I32, (BLOCKS, 1), 0).astype(I16)
    one, nought = BF16(1), BF16(0)

    ahead, behind = places(me, 1), places(me, -1)

    def to_peer(q, group):
        return pltpu.make_async_remote_copy(
            src_ref=sendbuf.at[q],
            dst_ref=recvbuf.at[me],
            send_sem=send_sem,
            recv_sem=recv_sems.at[group],
            device_id=(other, q),
            device_id_type=MESH,
        )

    def many(count, group):
        return pltpu.make_async_remote_copy(
            src_ref=sendbuf.at[pl.ds(0, count)],
            dst_ref=recvbuf.at[pl.ds(0, count)],
            send_sem=send_sem,
            recv_sem=recv_sems.at[group],
            device_id=(other, me),
            device_id_type=MESH,
        )

    def gather_one(q):
        cells = source[pl.ds(pl.multiple_of(q * CHUNKS, CHUNKS), CHUNKS), :]
        low, high = cells & (LANES - 1), cells >> 7
        used = jnp.where(
            slot < count[0, q],
            weight[pl.ds(pl.multiple_of(q * CHUNKS, CHUNKS), CHUNKS), :],
            0.0,
        )
        out = [jnp.zeros((8, LANES), F32) for _ in range(VARS)]
        for n in range(CHUNKS // 2):
            lows = jnp.concatenate([low[2 * n : 2 * n + 1], low[2 * n + 1 : 2 * n + 2]], axis=1)
            hot = jnp.where(lane_rows == lows.astype(I16), one, nought)
            rows = jnp.dot(
                table_halves,
                jnp.concatenate([hot, hot], axis=0),
                preferred_element_type=F32,
            )
            for half in range(2):
                c = 2 * n + half
                row = jnp.broadcast_to(high[c : c + 1], (8, LANES))
                within, group = row & 7, row >> 3
                for v in range(VARS):
                    picks = [
                        sublane_pick(
                            rows[
                                v * BLOCKS + t * 8 : v * BLOCKS + t * 8 + 8,
                                half * LANES : (half + 1) * LANES,
                            ],
                            within,
                        )
                        for t in range(BLOCKS // 8)
                    ]
                    pick = jnp.where(
                        group < 2,
                        jnp.where(group == 0, picks[0], picks[1]),
                        jnp.where(group == 2, picks[2], picks[3]),
                    )
                    out[v] = jnp.where(sublane == c, pick, out[v])
        for v in range(VARS):
            sendbuf[q, v * 8 : v * 8 + 8, :] = out[v] * used

    def gather(group, c_):
        peers = [peer_at(ahead, group, SENT, k) for k in range(SENT)]
        for q in peers:
            gather_one(q)

        @pl.when(group == 0)
        def _():
            pl.semaphore_wait(barrier, PEERS + 2)
            for halo in halos:
                halo.start()

        for q in peers:
            to_peer(q, lax.div(group, BATCH // SENT) + jnp.where(group == PEERS // SENT - 1, 1, 0)).start()
        return c_

    lax.fori_loop(0, PEERS // SENT, gather, 0)

    mixing_load.wait()
    spread = (
        lax.rem(lax.broadcasted_iota(I32, (ROWS, LEV), 0), LEV)
        == lax.broadcasted_iota(I32, (ROWS, LEV), 1)
    ).astype(F32)
    tiled = lax.dot_general(
        jnp.dot(spread, mixing[...], precision=lax.Precision.HIGHEST, preferred_element_type=F32),
        spread,
        (((1,), (1,)), ((), ())),
        precision=lax.Precision.HIGHEST,
        preferred_element_type=F32,
    )
    same = lax.div(lax.broadcasted_iota(I32, (ROWS, ROWS), 0), LEV) == lax.div(
        lax.broadcasted_iota(I32, (ROWS, ROWS), 1), LEV
    )
    mix_high, mix_low = halves(jnp.where(same, tiled, 0.0))
    mix_both = jnp.concatenate(
        [
            jnp.concatenate([mix_high, mix_high], axis=1),
            jnp.concatenate([mix_low, mix_low], axis=1),
        ],
        axis=0,
    )

    state_loads[1].wait()
    for halo in halos:
        halo.wait_recv()

    def blend(i, c_):
        cells = pl.ds(pl.multiple_of(i * 4 * LANES, 4 * LANES), 4 * LANES)
        both = jnp.concatenate(
            [halves(ext[v, :, cells])[part] for part in range(2) for v in range(VARS)], axis=0
        )
        result = jnp.dot(mix_both, both, preferred_element_type=F32)
        result = result[0:ROWS] + result[ROWS : 2 * ROWS]
        for v in range(VARS):
            blended[v, :, cells] = result[v * LEV : (v + 1) * LEV]
        high, low = halves(result)
        for e in range(4):
            at = pl.ds(pl.multiple_of((i * 4 + e) * ROWS, ROWS), ROWS)
            split[at, 0:LANES] = high[:, e * LANES : (e + 1) * LANES]
            split[at, LANES : 2 * LANES] = low[:, e * LANES : (e + 1) * LANES]
        return c_

    lax.fori_loop(0, (BLOCKS + SPAN - 1) // 4, blend, 0, unroll=9)
    for one_load in stencil_loads:
        one_load.wait()

    def rows_at(r, cells):
        return blended[r // 2, (r % 2) * 8 : (r % 2) * 8 + 8, cells]

    def stencil(b, c_):
        base = pl.multiple_of(b * LANES, LANES)
        window = split[pl.ds(pl.multiple_of(b * ROWS, ROWS), SPAN * ROWS), :]
        coefs = coef[:, pl.ds(base, LANES)]
        place = lane + nbr[:, pl.ds(base, LANES)]
        at, block = (place & (LANES - 1)), place >> 7
        rest = 1.0 - jnp.sum(coefs, axis=0, keepdims=True)
        acc = [rest * rows_at(r, pl.ds(HALO + base, LANES)) for r in range(ROWS // 8)]
        for pair in range(PRODUCTS // 2):
            hot = jnp.concatenate(
                [
                    jnp.where(lane_rows == at[j : j + 1].astype(I16), one, nought)
                    for j in (2 * pair, 2 * pair + 1)
                ],
                axis=1,
            )
            rows = jnp.dot(
                window, jnp.concatenate([hot, hot], axis=0), preferred_element_type=F32
            )
            for half in range(2):
                j = 2 * pair + half
                factor = jnp.broadcast_to(coefs[j : j + 1], (8, LANES))
                which = jnp.broadcast_to(block[j : j + 1], (8, LANES))
                lanes = slice(half * LANES, (half + 1) * LANES)
                for r in range(ROWS // 8):
                    pick = rows[r * 8 : r * 8 + 8, lanes]
                    for s in range(1, SPAN):
                        row = s * ROWS + r * 8
                        pick = jnp.where(which == s, rows[row : row + 8, lanes], pick)
                    acc[r] = acc[r] + factor * pick
        for r in range(ROWS // 8):
            mixed[r // 2, (r % 2) * 8 : (r % 2) * 8 + 8, pl.ds(base, LANES)] = acc[r]
        return c_

    lax.fori_loop(0, BLOCKS, stencil, 0, unroll=STENCIL_UNROLL)

    def permuted(b, rows):
        base = pl.multiple_of(b * LANES, LANES)
        cells = pl.ds(base, LANES)
        coefs = coef[:, cells]
        place = lane + nbr[:, cells]
        at, block = (place & (LANES - 1)), place >> 7
        acc = [mixed[r // 2, (r % 2) * 8 : (r % 2) * 8 + 8, cells] for r in rows]
        for j in range(PRODUCTS, NBR):
            turn = jnp.broadcast_to(at[j : j + 1], (8, LANES))
            which = jnp.broadcast_to(block[j : j + 1], (8, LANES))
            factor = jnp.broadcast_to(coefs[j : j + 1], (8, LANES))
            for i, r in enumerate(rows):
                pick = lane_pick(rows_at(r, cells), turn)
                for s in range(1, SPAN):
                    other_pick = lane_pick(rows_at(r, pl.ds(base + s * LANES, LANES)), turn)
                    pick = jnp.where(which == s, other_pick, pick)
                acc[i] = acc[i] + factor * pick
        for i, r in enumerate(rows):
            mixed[r // 2, (r % 2) * 8 : (r % 2) * 8 + 8, cells] = acc[i]

    target_load.wait()
    by_peer(raw_target, target)
    total[...] = jnp.zeros_like(total)

    def scatter_one(p):
        cells = target[pl.ds(pl.multiple_of(p * CHUNKS, CHUNKS), CHUNKS), :]
        low, high = (cells & (LANES - 1)), (cells >> 7)
        values, hots = [], []
        for c in range(CHUNKS):
            here = block_rows == high[c : c + 1].astype(I16)
            hots.append(jnp.where(lane_rows == low[c : c + 1].astype(I16), one, nought))
            parts = [halves(recvbuf[p, v * 8 + c : v * 8 + c + 1, :]) for v in range(VARS)]
            values.append(
                jnp.concatenate(
                    [jnp.where(here, parts[v][i], nought) for i in range(2) for v in range(VARS)],
                    axis=0,
                )
            )
        total[...] += lax.dot_general(
            jnp.concatenate(values, axis=1),
            jnp.concatenate(hots, axis=1),
            (((1,), (1,)), ((), ())),
            preferred_element_type=F32,
        )

    def store_of(group):
        width = CELLS * BATCH // PEERS
        cells = pl.ds(pl.multiple_of(group * width, width), width)
        return pltpu.make_async_copy(
            mixed.at[:, :, cells], mixed_hbm.at[:, :, cells], out_sems.at[group]
        )

    def arrived(group, batch, sem):
        peers = [peer_at(behind, group, batch, k) for k in range(batch)]
        many(batch, sem).wait_recv()
        half = ROWS // 16
        for k, p in enumerate(peers):
            scatter_one(p)
            permuted(group * (batch // 2) + k // 2, range(k % 2 * half, (k % 2 + 1) * half))

    last = PEERS // BATCH - 1

    def scatter(group, c_):
        arrived(group, BATCH, group)
        store_of(group).start()
        return c_

    lax.fori_loop(0, last, scatter, 0)

    def scatter_last(part, c_):
        arrived(part + last * (BATCH // SENT), SENT, part + last)
        return c_

    lax.fori_loop(0, BATCH // SENT, scatter_last, 0)
    store_of(last).start()

    for v in range(VARS):
        for b in range(BLOCKS):
            r = v * BLOCKS + b
            flux[v : v + 1, b * LANES : (b + 1) * LANES] = (
                total[r : r + 1, :] + total[r + VARS * BLOCKS : r + VARS * BLOCKS + 1, :]
            )

    flux_store = pltpu.make_async_copy(flux, flux_hbm, flux_sem)
    flux_store.start()

    many(PEERS, 0).wait_send()
    for halo in halos:
        halo.wait_send()
    for group in range(PEERS // BATCH):
        store_of(group).wait()
    flux_store.wait()


def finish(
    mixed_hbm, flux_in, mixing_hbm, updated_hbm, flux_out, state, flux, mixing, load_sems, store_sems
):
    loads = [
        pltpu.make_async_copy(mixed_hbm.at[v], state.at[v], load_sems.at[v]) for v in range(VARS)
    ]
    flux_load = pltpu.make_async_copy(flux_in, flux, load_sems.at[VARS])
    mixing_load = pltpu.make_async_copy(mixing_hbm.at[0], mixing, load_sems.at[VARS + 1])
    for load in [flux_load, mixing_load, *loads]:
        load.start()
    flux_load.wait()
    mixing_load.wait()
    flux_store = pltpu.make_async_copy(flux, flux_out.at[0], store_sems.at[VARS])
    flux_store.start()
    stores = []
    shares = [
        jnp.broadcast_to(mixing[h * 8 : h * 8 + 8, 0:1], (8, LANES)) for h in range(LEV // 8)
    ]
    for v in range(VARS):
        loads[v].wait()
        for b in range(BLOCKS):
            cells = slice(b * LANES, (b + 1) * LANES)
            row = jnp.broadcast_to(flux[v : v + 1, cells], (8, LANES))
            for h in range(LEV // 8):
                levels = slice(h * 8, h * 8 + 8)
                state[v, levels, cells] = state[v, levels, cells] + shares[h] * row
        store = pltpu.make_async_copy(state.at[v], updated_hbm.at[0, v], store_sems.at[v])
        store.start()
        stores.append(store)
    for store in stores:
        store.wait()
    flux_store.wait()


def local(
    model_state,
    neighbours,
    stencil_coef,
    column_mixing_operator,
    remap_count,
    remap_source,
    remap_weight,
    remap_target,
):
    hbm = pl.BlockSpec(memory_space=pltpu.HBM)
    mixed, flux = pl.pallas_call(
        kernel,
        out_shape=(
            jax.ShapeDtypeStruct((VARS, LEV, CELLS), F32),
            jax.ShapeDtypeStruct((VARS, CELLS), F32),
        ),
        in_specs=[hbm] * 8,
        out_specs=(hbm, hbm),
        scratch_shapes=[
            pltpu.VMEM((VARS, LEV, CELLS + 2 * HALO), F32),
            pltpu.VMEM((VARS, LEV, CELLS + 2 * HALO), F32),
            pltpu.VMEM((LEV, LEV), F32),
            pltpu.SMEM((1, PEERS), I32),
            pltpu.VMEM((VARS, CELLS), F32),
            pltpu.VMEM((NBR, CELLS), I32),
            pltpu.VMEM((NBR, CELLS), F32),
            pltpu.VMEM((PEERS, CAP), I32),
            pltpu.VMEM((PEERS, CAP), F32),
            pltpu.VMEM((PEERS, CAP), I32),
            pltpu.VMEM((PEERS * CHUNKS, LANES), I32),
            pltpu.VMEM((PEERS * CHUNKS, LANES), F32),
            pltpu.VMEM((PEERS * CHUNKS, LANES), I32),
            pltpu.VMEM((VARS * BLOCKS, LANES), F32),
            pltpu.VMEM((PEERS, VARS * CHUNKS, LANES), F32),
            pltpu.VMEM((PEERS, VARS * CHUNKS, LANES), F32),
            pltpu.VMEM(((BLOCKS + SPAN - 1) * ROWS, 2 * LANES), BF16),
            pltpu.VMEM((VARS, LEV, CELLS), F32),
            pltpu.VMEM((2 * VARS * BLOCKS, LANES), F32),
            pltpu.SemaphoreType.DMA((9,)),
            pltpu.SemaphoreType.DMA((2,)),
            pltpu.SemaphoreType.DMA((2,)),
            pltpu.SemaphoreType.DMA,
            pltpu.SemaphoreType.DMA((PEERS // BATCH + 1,)),
            pltpu.SemaphoreType.DMA((PEERS // BATCH,)),
            pltpu.SemaphoreType.DMA,
        ],
        compiler_params=pltpu.CompilerParams(
            collective_id=0, has_side_effects=True, vmem_limit_bytes=60 << 20
        ),
        name="step",
    )(
        model_state,
        neighbours,
        stencil_coef,
        column_mixing_operator,
        remap_count,
        remap_source,
        remap_weight,
        remap_target,
    )
    return pl.pallas_call(
        finish,
        out_shape=(
            jax.ShapeDtypeStruct((1, VARS, LEV, CELLS), F32),
            jax.ShapeDtypeStruct((1, VARS, CELLS), F32),
        ),
        in_specs=[hbm] * 3,
        out_specs=(hbm, hbm),
        scratch_shapes=[
            pltpu.VMEM((VARS, LEV, CELLS), F32),
            pltpu.VMEM((VARS, CELLS), F32),
            pltpu.VMEM((LEV, LEV), F32),
            pltpu.SemaphoreType.DMA((VARS + 2,)),
            pltpu.SemaphoreType.DMA((VARS + 1,)),
        ],
        compiler_params=pltpu.CompilerParams(vmem_limit_bytes=60 << 20),
        name="finish",
    )(mixed, flux, column_mixing_operator)


def solution(mesh):
    in_specs = (
        P("comp", None, None, "dom"),
        P("comp", None, "dom"),
        P("comp", None, "dom"),
        P("comp", None, None),
        P("comp", "dom", None),
        P("comp", "dom", None, None),
        P("comp", "dom", None, None),
        P("comp", "dom", None, None),
    )
    out_specs = (P("comp", None, None, "dom"), P("comp", None, "dom"))
    return jax.shard_map(local, mesh=mesh, in_specs=in_specs, out_specs=out_specs, check_vma=False)
```
